128 devices in a mesh: row: 16 (over x, y_hi, core), col: 8 (over y_lo, z).
Axes of the slice: x: 4, y: 4 (y_hi: 2, y_lo: 2; y = y_hi * 2 + y_lo), z: 4, core: 2. Of those that a mesh axis runs over, the one named last changes fastest.
Arguments:
- z_rows: bfloat16 [16, 2048, 128], P('row', 'col'), may hold values from -6 to 6
- z_cols: bfloat16 [16, 2048, 128], P('row', 'col'), may hold values from -6 to 6
- bias_start: bfloat16 [4, 2048, 2048], P(None, 'row', 'col'), may hold values from -6 to 325, as said below
- bias_end: bfloat16 [4, 2048, 2048], P(None, 'row', 'col'), may hold values from -6 to 325, as said below
- w_start_in: bfloat16 [128, 512], replicated, may hold values from -0.5 to 0.5
- w_start_out: bfloat16 [128, 128], replicated, may hold values from -2 to 2
- w_end_in: bfloat16 [128, 512], replicated, may hold values from -0.5 to 0.5
- w_end_out: bfloat16 [128, 128], replicated, may hold values from -2 to 2
- token_mask: int32 [2048], replicated, may hold values 0 or 1
- offsets: int32 [2], replicated, may hold values from 0 to 2032
Outputs:
- out_start: bfloat16 [16, 2048, 128], P('col', 'row')
- out_end: bfloat16 [16, 2048, 128], P('row', 'col')
The draws below stay inside these ranges and needn't reach their ends.
Inputs may be any that keep to these rules, and one draw needn't show every extreme that they name: `bias_start`: entry [h, j, k] belongs to the pair (j, k). `bias_end`: entry [h, k, i] belongs to the pair (k, i).
All inputs are finite; a program needn't handle non-finite values.
Results may differ from the reference program's by a relative error of at most 0.0082.
Values may be sent and summed in bfloat16 or wider, within the bound.
A program may use at most 128 MiB of HBM per device.

```python
import jax
import jax.numpy as jnp
from jax import lax

C = 128
H = 4
DH = 32
SLAB = 16
TILE = 128
N = 2048
N_ROW = 16
N_COL = 8


def spiked(key, spike_rate):
    base_key, hit_key, level_key, step_key = jax.random.split(key, 4)
    background = jnp.clip(2.0 * jax.random.normal(base_key, (H, N, N), jnp.float32), -6.0, 6.0)
    hit_mask = jax.random.uniform(hit_key, (H, N, N), jnp.float32) < spike_rate / N
    levels = jax.random.randint(level_key, (H, N, N), 1, 4).astype(jnp.float32)
    step_values = jax.random.randint(step_key, (H, N, N), 0, 2).astype(jnp.float32)
    peak_values = 100.0 * levels + 20.0 + 2.0 * step_values + 0.5 * background
    return jnp.where(hit_mask, peak_values, background).astype(jnp.bfloat16)


def draw_bias_start(key, part):
    key = jax.random.fold_in(key, 11)
    return spiked(key, 0.0)


def draw_bias_end(key, part):
    key = jax.random.fold_in(key, 23)
    return spiked(key, 0.0)


def with_ends(entries, rng, least, high):
    place = [jax.random.randint(jax.random.fold_in(rng, axis), (), 0, length) for axis, length in enumerate(entries.shape)]
    widest = entries.shape.index(max(entries.shape))
    next_to = place[:widest] + [(place[widest] + 1) % entries.shape[widest]] + place[widest + 1:]
    return entries.at[tuple(place)].set(least).at[tuple(next_to)].set(high)


def level_of(own_key, dims, shards, low, high):
    factor_of = 1.0
    for axis_at, blocks in shards:
        steps = jax.random.uniform(jax.random.fold_in(jax.random.fold_in(own_key, 6), axis_at), (blocks,), jnp.float32, low / len(shards), high / len(shards))
        factor_of = factor_of * jnp.repeat(jnp.exp(steps), dims[axis_at] // blocks).reshape((-1,) + (1,) * (len(dims) - 1 - axis_at))
    return factor_of


def noise(stream_key, extent, scale, most, cuts=(), held_as=jnp.bfloat16):
    array = scale * jax.random.normal(stream_key, extent, jnp.float32)
    if cuts:
        array = array * level_of(stream_key, extent, cuts, -0.22, 0.18)
    return jnp.clip(array, -most, most).astype(held_as)


def setup_inputs(seed: int = 0) -> dict:
    key_list = jax.random.split(jax.random.key(seed), 11)
    z_rows = noise(key_list[0], (SLAB, N, C), 1.0, 6.0, ((0, 16), (1, 8)))
    z_cols = noise(key_list[1], (SLAB, N, C), 1.0, 6.0, ((0, 16), (1, 8)))
    bias_start = draw_bias_start(jax.random.fold_in(key_list[10], 71), 0)
    bias_end = draw_bias_end(jax.random.fold_in(key_list[10], 71), 0)
    w_start_in = noise(key_list[4], (C, 4 * C), C ** -0.5, 0.5)
    w_start_out = noise(key_list[5], (C, C), 0.35, 2.0)
    w_end_in = noise(key_list[6], (C, 4 * C), C ** -0.5, 0.5)
    w_end_out = noise(key_list[7], (C, C), 0.35, 2.0)
    token_mask = with_ends((jax.random.randint(key_list[8], (N,), 0, 8) < 7).astype(jnp.int32), jax.random.fold_in(key_list[8], 1), 0, 1)
    offsets = jax.random.randint(key_list[9], (2,), 0, N - SLAB + 1).astype(jnp.int32)
    return {"z_rows": z_rows, "z_cols": z_cols, "bias_start": bias_start, "bias_end": bias_end, "w_start_in": w_start_in, "w_start_out": w_start_out, "w_end_in": w_end_in, "w_end_out": w_end_out, "token_mask": token_mask, "offsets": offsets}


def normalize(pair_block):
    values = pair_block.astype(jnp.float32)
    center = values - lax.optimization_barrier(jnp.mean(values, axis=-1, keepdims=True))
    spread = lax.optimization_barrier(jnp.mean(center * center, axis=-1, keepdims=True))
    return (center * lax.rsqrt(spread + 1e-05)).astype(jnp.bfloat16)

def project(normed, weights, column, factor):
    chosen = weights[:, column * C:(column + 1) * C]
    result = jnp.dot(normed.reshape(-1, C), chosen, preferred_element_type=jnp.float32)
    return result.reshape(normed.shape[:-1] + (C,)) * factor

def start_row(query_row, key_row, value_row, bias_start, key_bias):
    scores = jnp.einsum('bhd,khd->hbk', query_row.astype(jnp.float32), key_row.astype(jnp.float32))
    scores = scores + bias_start.astype(jnp.float32) + key_bias
    grouped = scores.reshape(H, N, N_COL, N // N_COL)
    maxima = lax.optimization_barrier(jnp.max(grouped, axis=-1))
    exponent = jnp.exp(grouped - maxima[..., None])
    denominator = lax.optimization_barrier(jnp.sum(exponent, axis=-1))
    rounded = lax.optimization_barrier(exponent.astype(jnp.bfloat16)).astype(jnp.float32)
    grouped_values = value_row.astype(jnp.float32).reshape(N_COL, N // N_COL, H, DH)
    numerator = jnp.einsum('hbgk,gkhd->hbgd', rounded, grouped_values)
    largest = lax.optimization_barrier(jnp.max(maxima, axis=-1, keepdims=True))
    factor = jnp.exp(maxima - largest)
    result = lax.optimization_barrier(jnp.sum(numerator * factor[..., None], axis=2)) / lax.optimization_barrier(jnp.sum(denominator * factor, axis=-1))[..., None]
    return jnp.transpose(result, (1, 0, 2)).reshape(N, C)

def end_row(query_row, key_row, value_row, bias_end, key_bias):
    scores = jnp.einsum('khd,bhd->hkb', key_row.astype(jnp.float32), query_row.astype(jnp.float32))
    scores = scores + bias_end.astype(jnp.float32) + key_bias[:, None]
    grouped = scores.reshape(H, N_ROW, TILE, N)
    maxima = lax.optimization_barrier(jnp.max(grouped, axis=2))
    exponent = jnp.exp(grouped - maxima[:, :, None, :])
    denominator = lax.optimization_barrier(jnp.sum(exponent, axis=2))
    rounded = lax.optimization_barrier(exponent.astype(jnp.bfloat16)).astype(jnp.float32)
    grouped_values = value_row.astype(jnp.float32).reshape(N_ROW, TILE, H, DH)
    numerator = jnp.einsum('hgkb,gkhd->hgbd', rounded, grouped_values)
    largest = lax.optimization_barrier(jnp.max(maxima, axis=1, keepdims=True))
    factor = jnp.exp(maxima - largest)
    result = lax.optimization_barrier(jnp.sum(numerator * factor[..., None], axis=1)) / lax.optimization_barrier(jnp.sum(denominator * factor, axis=1))[..., None]
    return jnp.transpose(result, (1, 0, 2)).reshape(N, C)

def finish(attended, gate_values, out_weight, row_mask, column_mask):
    gated_rows = (jax.nn.sigmoid(gate_values) * attended).astype(jnp.bfloat16)
    result = jnp.dot(gated_rows.reshape(-1, C), out_weight, preferred_element_type=jnp.float32)
    result = result.reshape(gated_rows.shape)
    return (result * (row_mask[:, None] * column_mask[None, :])[..., None]).astype(jnp.bfloat16)

def reference(z_rows, z_cols, bias_start, bias_end, w_start_in, w_start_out, w_end_in, w_end_out, token_mask, offsets):
    mask_float = token_mask.astype(jnp.float32)
    key_bias = (mask_float - 1.0) * 1000000000.0
    query_scale = DH ** (-0.5)
    normed_rows = normalize(z_rows)
    normed_cols = normalize(z_cols)
    query_start = project(normed_rows, w_start_in, 0, query_scale).astype(jnp.bfloat16).reshape(SLAB, N, H, DH)
    keys_start = project(normed_rows, w_start_in, 1, 1.0).astype(jnp.bfloat16).reshape(SLAB, N, H, DH)
    values_start = project(normed_rows, w_start_in, 2, 1.0).astype(jnp.bfloat16).reshape(SLAB, N, H, DH)
    gate_start = project(normed_rows, w_start_in, 3, 1.0)
    attend_start = lax.map(lambda block_items: start_row(block_items[0], block_items[1], block_items[2], bias_start, key_bias), (query_start, keys_start, values_start))
    row_mask = lax.dynamic_slice_in_dim(mask_float, offsets[0], SLAB)
    out_start = finish(attend_start, gate_start, w_start_out, row_mask, mask_float)
    query_end = project(normed_cols, w_end_in, 0, query_scale).astype(jnp.bfloat16).reshape(SLAB, N, H, DH)
    keys_end = project(normed_cols, w_end_in, 1, 1.0).astype(jnp.bfloat16).reshape(SLAB, N, H, DH)
    values_end = project(normed_cols, w_end_in, 2, 1.0).astype(jnp.bfloat16).reshape(SLAB, N, H, DH)
    gate_end = project(normed_cols, w_end_in, 3, 1.0)
    attend_end = lax.map(lambda block_items: end_row(block_items[0], block_items[1], block_items[2], bias_end, key_bias), (query_end, keys_end, values_end))
    end_mask = lax.dynamic_slice_in_dim(mask_float, offsets[1], SLAB)
    out_end = finish(attend_end, gate_end, w_end_out, end_mask, mask_float)
    return (out_start, out_end)
```

```python
import functools
import math

import jax
import jax.numpy as jnp
from jax import lax
from jax.experimental import pallas as pl
from jax.experimental.pallas import tpu as pltpu
from jax.sharding import PartitionSpec as P

MESH = pl.DeviceIdType.MESH
LOG2E = math.log2(math.e)
LOOK = 2
F32 = jnp.float32
BF16 = jnp.bfloat16


def nn(a, b):
    return lax.dot_general(a, b, (((1,), (0,)), ((), ())), preferred_element_type=F32)


def nt(a, b):
    return lax.dot_general(a, b, (((1,), (1,)), ((), ())), preferred_element_type=F32)


def normalize(block):
    values = block.astype(F32)
    center = values - jnp.mean(values, axis=-1, keepdims=True)
    spread = jnp.mean(center * center, axis=-1, keepdims=True)
    return (center * lax.rsqrt(spread + 1e-05)).astype(BF16)


def kernel(
    n, nc, heads,
    zr, zc, bs, be, ws, wso, we, weo, tm, tms, offs,
    out_s, out_e,
    x, kv, q, bias, wvt, wgt, be_in, pn, pst, rsn, rss, ren, res,
    sg, sn, sf, spn, sps, sb,
    rg, rn, rf, rsn_sem, rss_sem, ren_sem, res_sem, rb,
):
    r = lax.axis_index("row")
    c = lax.axis_index("col")
    core = lax.rem(r, 2)
    chip = r // 2
    mate = r + 1 - 2 * core
    tile = tm.shape[1]
    channels = zr.shape[2]
    depth = channels // heads
    per = n // nc
    mine = pl.ds(pl.multiple_of(core * tile, tile), tile)
    other = pl.ds(pl.multiple_of((1 - core) * tile, tile), tile)
    diagonal = chip == c

    def peer(u):
        return lax.rem((r + 1) // 2 + u + nc - c, nc)

    def turn(t):
        return lax.rem(2 * (chip + c) + 2 * n - t, n)

    barrier = pltpu.get_barrier_semaphore()

    def greet(row, col):
        pl.semaphore_signal(barrier, inc=1, device_id=(row, col), device_id_type=MESH)

    def greet_row(d, carry):
        greet(lax.rem(r + d, n), c)
        return carry

    def greet_col(d, carry):
        greet(r, lax.rem(c + d, nc))
        return carry

    lax.fori_loop(1, n, greet_row, 0)
    lax.fori_loop(1, nc, greet_col, 0)

    def greet_near(d, carry):
        row_to, col_to = 2 * c + lax.rem(d, 2), d // 2
        @pl.when(jnp.logical_not((row_to == r) & (col_to == c)))
        def _():
            greet(row_to, col_to)
        @pl.when(jnp.logical_not((d == r) & diagonal))
        def _():
            greet(d, chip)
        return carry

    lax.fori_loop(0, n, greet_near, 0)

    x[0] = normalize(zr[0])
    x[1] = normalize(zc[0])

    pl.semaphore_wait(barrier, n - 1 + nc - 1 + 2 * n - jnp.where(diagonal, 2, 0))

    def half(form, e):
        return x.at[form, pl.ds(e * tile, tile)]

    def gather_copy(form, row_to, e):
        if form == 0:
            dst = kv.at[0, r, pl.ds(e * tile, tile)]
        else:
            dst = q.at[1, r]
        return half(form, e), dst, sg.at[form, row_to], rg.at[form, r]

    def near_copy(form, col_to, e):
        if form == 0:
            dst = q.at[0, r]
        else:
            dst = kv.at[1, r, pl.ds(e * tile, tile)]
        return half(form, e), dst, sn.at[form, 2 * col_to + e], rn.at[form, r]

    def remote(src, dst, send, recv, row, col):
        return pltpu.make_async_remote_copy(
            src_ref=src, dst_ref=dst, send_sem=send, recv_sem=recv,
            device_id=(row, col), device_id_type=MESH,
        )

    def either(here, src, dst, send, recv, row, col):
        @pl.when(here)
        def _():
            pltpu.make_async_copy(src, dst, recv).start()
        @pl.when(jnp.logical_not(here))
        def _():
            remote(src, dst, send, recv, row, col).start()

    def sent(here, src, dst, send, recv):
        @pl.when(jnp.logical_not(here))
        def _():
            remote(src, dst, send, recv, mate, c).wait_send()

    bias_swap = remote(
        be.at[:, :, pl.ds(pl.multiple_of((1 - core) * tile, tile), tile)], be_in, sb, rb, mate, c
    )

    def send_form(form):
        def step(u, carry):
            to = peer(u)
            for e in range(2):
                either(2 * to + e == r, *gather_copy(form, 2 * to + e, e), 2 * to + e, c)
                here = (2 * c + e == r) & (to == c)
                either(here, *near_copy(form, to, e), 2 * c + e, to)
            return carry
        lax.fori_loop(0, nc, step, 0)

    def drain_form(form):
        def step(u, carry):
            for e in range(2):
                sent(2 * u + e == r, *gather_copy(form, 2 * u + e, e))
                sent((2 * c + e == r) & (u == c), *near_copy(form, u, e))
            return carry
        lax.fori_loop(0, nc, step, 0)

    send_form(0)
    bias_swap.start()
    send_form(1)

    for form, w in enumerate((ws, we)):
        wvt[form] = w[:, 2 * channels : 3 * channels].astype(F32).T.astype(BF16)
        wgt[form] = w[:, 3 * channels : 4 * channels].astype(F32).T.astype(BF16)

    def mask_row(t):
        return tm[pl.ds(t, 1), :].astype(F32)

    def penalty(t):
        return (mask_row(t) - 1.0) * 1e9

    for g in range(2):
        row_bias = penalty(2 * c + g)
        for h in range(heads):
            part = (bs[h, :, g * tile : (g + 1) * tile].astype(F32) + row_bias) * LOG2E
            bias[0, h, g * tile : (g + 1) * tile, :] = part.T

    bias_swap.wait_recv()
    for part_ref, rows, t in (
        (be.at[:, :, mine], mine, r),
        (be_in, other, mate),
    ):
        column = jnp.broadcast_to(penalty(t), (tile, tile)).T
        for h in range(heads):
            bias[1, h, rows, :] = (part_ref[h].astype(F32) + column) * LOG2E

    scale = depth ** (-0.5) * LOG2E
    lane = lax.broadcasted_iota(jnp.int32, (tile, channels), 1) // depth
    ones = jnp.ones((16, 2 * tile), BF16)

    def attend(form, w, a):
        rows = kv[form, a]
        keys = nn(rows, w[:, channels : 2 * channels]).astype(BF16)
        values = nt(wvt[form], rows).astype(BF16)
        query = nn(q[form, a], w[:, :channels]) * scale
        for h in range(heads):
            chosen = jnp.where(lane == h, query, 0.0).astype(BF16)
            scores = nt(keys, chosen) + bias[form, h]
            peak = jnp.max(scores, axis=0, keepdims=True)
            probs = jnp.exp2(scores - peak).astype(BF16)
            lhs = jnp.concatenate([values[h * depth : (h + 1) * depth], ones], axis=0)
            total = nn(lhs, probs)
            pn[form, a, h * depth : (h + 1) * depth, :] = total[:depth].astype(BF16)
            pst[form, a, h : h + 1, :] = peak
            pst[form, a, heads + h : heads + h + 1, :] = total[depth : depth + 1]

    def landed(dst, recv):
        remote(dst, dst, sf.at[0, 0], recv, mate, c).wait_recv()

    own_sem = (rg, rn)
    far_sem = (rn, rg)

    def forward(form, a):
        piece = kv.at[form, a, mine]
        landed(piece, own_sem[form].at[form, a])
        remote(piece, piece, sf.at[form, a], rf.at[form, a], mate, c).start()

    def partial_copies(form, a):
        src_n, src_s = pn.at[form, a], pst.at[form, a]
        sems = (spn.at[form, a], sps.at[form, a])
        if form == 0:
            to, b = a // per, lax.rem(a, per)
            return (
                to == c, r, to,
                (src_n, rsn.at[c, b], sems[0], rsn_sem.at[c, b]),
                (src_s, rss.at[c, b], sems[1], rss_sem.at[c, b]),
            )
        return (
            a == r, a, c,
            (src_n, ren.at[r], sems[0], ren_sem.at[r]),
            (src_s, res.at[r], sems[1], res_sem.at[r]),
        )

    def run_form(form, w):
        look = LOOK if form == 0 else n

        def ahead(t, carry):
            forward(form, turn(t))
            return carry

        lax.fori_loop(0, look, ahead, 0)

        def step(t, carry):
            a = turn(t)
            if look < n:
                @pl.when(t + look < n)
                def _():
                    forward(form, turn(t + look))
            landed(q.at[form, a], far_sem[form].at[form, a])
            landed(kv.at[form, a, other], rf.at[form, a])
            attend(form, w, a)
            here, row, col, numer, stats = partial_copies(form, a)
            either(here, *numer, row, col)
            either(here, *stats, row, col)
            return carry

        lax.fori_loop(0, n, step, 0)

    def combine(parts, stats):
        peaks = [s[:heads] for s in stats]
        largest = functools.reduce(jnp.maximum, peaks)
        factors = [jnp.exp2(p - largest) for p in peaks]
        denom = sum(f * s[heads:] for f, s in zip(factors, stats))
        rows = []
        for h in range(heads):
            pick = slice(h * depth, (h + 1) * depth)
            total = sum(f[h : h + 1] * p[pick].astype(F32) for f, p in zip(factors, parts))
            rows.append(total / denom[h : h + 1])
        return jnp.concatenate(rows, axis=0)

    def finish(form, attended, rows, weight, mask):
        gate = nt(wgt[form], rows)
        gated = jax.nn.sigmoid(gate) * attended * mask
        return nn(gated.T.astype(BF16), weight).astype(BF16)

    run_form(0, ws)
    run_form(1, we)

    for b in range(per):
        a = per * c + b
        for g in range(nc):
            landed(rsn.at[g, b], rsn_sem.at[g, b])
            landed(rss.at[g, b], rss_sem.at[g, b])
        attended = combine([rsn[g, b] for g in range(nc)], [rss[g, b] for g in range(nc)])
        mask = mask_row(r) * tms[offs[0] + a].astype(F32)
        out_s[b] = finish(0, attended, q[0, a], wso[...], mask)

    for e in range(2):
        for m in range(nc):
            landed(ren.at[2 * m + e], ren_sem.at[2 * m + e])
            landed(res.at[2 * m + e], res_sem.at[2 * m + e])
        attended = combine(
            [ren[2 * m + e] for m in range(nc)], [res[2 * m + e] for m in range(nc)]
        )
        mask = mask_row(2 * c + e) * tms[offs[1] + r].astype(F32)
        rows = x[1, e * tile : (e + 1) * tile, :]
        out_e[0, e * tile : (e + 1) * tile, :] = finish(1, attended, rows, weo[...], mask)

    bias_swap.wait_send()
    for form in range(2):
        drain_form(form)

        def drain(a, carry):
            piece = kv.at[form, a, mine]
            remote(piece, piece, sf.at[form, a], rf.at[form, a], mate, c).wait_send()
            here, _, _, numer, stats = partial_copies(form, a)
            sent(here, *numer)
            sent(here, *stats)
            return carry

        lax.fori_loop(0, n, drain, 0)


def local(z_rows, z_cols, bias_start, bias_end, w_start_in, w_start_out, w_end_in, w_end_out, token_mask, offsets):
    n, nc = lax.axis_size("row"), lax.axis_size("col")
    heads, tile, span = bias_start.shape
    channels = z_rows.shape[2]
    per = n // nc
    vmem = pl.BlockSpec(memory_space=pltpu.VMEM)
    smem = pl.BlockSpec(memory_space=pltpu.SMEM)
    dma = pltpu.SemaphoreType.DMA
    return pl.pallas_call(
        functools.partial(kernel, n, nc, heads),
        out_shape=(
            jax.ShapeDtypeStruct((per, tile, channels), BF16),
            jax.ShapeDtypeStruct((1, span, channels), BF16),
        ),
        in_specs=[vmem] * 9 + [smem] * 2,
        out_specs=(vmem, vmem),
        scratch_shapes=[
            pltpu.VMEM((2, span, channels), BF16),
            pltpu.VMEM((2, n, span, channels), BF16),
            pltpu.VMEM((2, n, tile, channels), BF16),
            pltpu.VMEM((2, heads, span, tile), F32),
            pltpu.VMEM((2, channels, channels), BF16),
            pltpu.VMEM((2, channels, channels), BF16),
            pltpu.VMEM((heads, tile, tile), BF16),
            pltpu.VMEM((2, n, channels, tile), BF16),
            pltpu.VMEM((2, n, 2 * heads, tile), F32),
            pltpu.VMEM((nc, per, channels, tile), BF16),
            pltpu.VMEM((nc, per, 2 * heads, tile), F32),
            pltpu.VMEM((n, channels, tile), BF16),
            pltpu.VMEM((n, 2 * heads, tile), F32),
            dma((2, n)), dma((2, n)), dma((2, n)), dma((2, n)), dma((2, n)), dma,
            dma((2, n)), dma((2, n)), dma((2, n)),
            dma((nc, per)), dma((nc, per)), dma((n,)), dma((n,)), dma,
        ],
        compiler_params=pltpu.CompilerParams(
            collective_id=0, has_side_effects=True, vmem_limit_bytes=32 * 1024 * 1024
        ),
        name="triangle_attention",
    )(
        z_rows, z_cols, bias_start, bias_end, w_start_in, w_start_out, w_end_in, w_end_out,
        token_mask.reshape(-1, tile), token_mask, offsets,
    )


def solution(mesh):
    return jax.shard_map(
        local,
        mesh=mesh,
        in_specs=(
            P("row", "col", None),
            P("row", "col", None),
            P(None, "row", "col"),
            P(None, "row", "col"),
            P(),
            P(),
            P(),
            P(),
            P(),
            P(),
        ),
        out_specs=(P("col", "row", None), P("row", "col", None)),
        check_vma=False,
    )
```

```python
import functools
import math

import jax
import jax.numpy as jnp
from jax import lax
from jax.experimental import pallas as pl
from jax.experimental.pallas import tpu as pltpu
from jax.sharding import PartitionSpec as P

MESH = pl.DeviceIdType.MESH
LOG2E = math.log2(math.e)
LOOK = 2
F32 = jnp.float32
BF16 = jnp.bfloat16


def nn(a, b):
    return lax.dot_general(a, b, (((1,), (0,)), ((), ())), preferred_element_type=F32)


def nt(a, b):
    return lax.dot_general(a, b, (((1,), (1,)), ((), ())), preferred_element_type=F32)


def normalize(block):
    values = block.astype(F32)
    center = values - jnp.mean(values, axis=-1, keepdims=True)
    spread = jnp.mean(center * center, axis=-1, keepdims=True)
    return (center * lax.rsqrt(spread + 1e-05)).astype(BF16)


def kernel(
    n, nc, heads,
    zr, zc, bs, be, ws, wso, we, weo, tm, tms, offs,
    out_s, out_e,
    cols, kv, q, bias, wvt, wgt, be_in, pn, pst, rsn, rss, ren, res,
    sg, sn, sc, sz, sf, spn, sps, sb,
    rg, rn, rc, rf, rsn_sem, rss_sem, ren_sem, res_sem, rb,
):
    r = lax.axis_index("row")
    c = lax.axis_index("col")
    core = lax.rem(r, 2)
    chip = r // 2
    mate = r + 1 - 2 * core
    tile = tm.shape[1]
    channels = zr.shape[2]
    depth = channels // heads
    per = n // nc
    mine = pl.ds(pl.multiple_of(core * tile, tile), tile)
    other = pl.ds(pl.multiple_of((1 - core) * tile, tile), tile)
    deep = nc // 2
    lap, lane_z = c // deep, lax.rem(c, deep)
    twin = (1 - lap) * deep + lane_z

    def level(d):
        return lap * deep + lax.rem(lane_z + d, deep)

    def turn(t):
        return 2 * lax.rem(chip + nc - t // 2, nc) + lax.rem(t, 2)

    barrier = pltpu.get_barrier_semaphore()

    def greet(row, col):
        pl.semaphore_signal(barrier, inc=1, device_id=(row, col), device_id_type=MESH)

    def greet_row(d, carry):
        greet(lax.rem(r + d, n), c)
        return carry

    def greet_col(d, carry):
        greet(r, lax.rem(c + d, nc))
        return carry

    lax.fori_loop(1, n, greet_row, 0)
    lax.fori_loop(1, nc, greet_col, 0)

    cols[0, c] = normalize(zr[0])
    cols[1, c] = normalize(zc[0])

    pl.semaphore_wait(barrier, n - 1 + nc - 1)

    def half(form, block, e):
        return cols.at[form, block, pl.ds(e * tile, tile)]

    def gather_copy(form, to, e):
        if form == 0:
            dst = kv.at[0, r, pl.ds(e * tile, tile)]
        else:
            dst = q.at[1, r]
        return half(form, c, e), dst, sg.at[form, 2 * to + e], rg.at[form, r]

    def near_copy(form, to, e):
        if form == 0:
            dst = q.at[0, r]
        else:
            dst = kv.at[1, r, pl.ds(e * tile, tile)]
        return half(form, to, e), dst, sn.at[form, 2 * to + e], rn.at[form, r]

    def remote(src, dst, send, recv, row, col):
        return pltpu.make_async_remote_copy(
            src_ref=src, dst_ref=dst, send_sem=send, recv_sem=recv,
            device_id=(row, col), device_id_type=MESH,
        )

    def either(here, src, dst, send, recv, row, col):
        @pl.when(here)
        def _():
            pltpu.make_async_copy(src, dst, recv).start()
        @pl.when(jnp.logical_not(here))
        def _():
            remote(src, dst, send, recv, row, col).start()

    def sent(here, src, dst, send, recv):
        @pl.when(jnp.logical_not(here))
        def _():
            remote(src, dst, send, recv, mate, c).wait_send()

    bias_swap = remote(
        be.at[:, :, pl.ds(pl.multiple_of((1 - core) * tile, tile), tile)], be_in, sb, rb, mate, c
    )

    def along(u):
        return lax.rem(chip + u, nc)

    def column_copies(form):
        mine_out = [(twin, sc.at[form, 0])] + [(level(d), sc.at[form, d]) for d in range(1, deep)]
        own = cols.at[form, c]
        return [remote(own, own, sem, rc.at[form, c], r, to) for to, sem in mine_out]

    def relay_copies(form):
        other_block = cols.at[form, twin]
        return [
            remote(other_block, other_block, sz.at[form, d], rc.at[form, twin], r, level(d))
            for d in range(1, deep)
        ]

    def relay(form):
        landed(cols.at[form, twin], rc.at[form, twin])
        for copy in relay_copies(form):
            copy.start()

    def send_gather(form):
        def step(u, carry):
            to = along(u)
            for e in range(2):
                either((u == 0) & (core == e), *gather_copy(form, to, e), 2 * to + e, c)
            return carry
        lax.fori_loop(0, nc, step, 0)

    def send_near(form, u):
        to = along(u)
        @pl.when((to != c) & (to != twin))
        def _():
            landed(cols.at[form, to], rc.at[form, to])
        for e in range(2):
            either((u == 0) & (core == e), *near_copy(form, to, e), 2 * to + e, c)

    def drain_form(form):
        for copy in column_copies(form) + relay_copies(form):
            copy.wait_send()
        def step(u, carry):
            to = along(u)
            for e in range(2):
                here = (u == 0) & (core == e)
                sent(here, *gather_copy(form, to, e))
                sent(here, *near_copy(form, to, e))
            return carry
        lax.fori_loop(0, nc, step, 0)

    def landed(dst, recv):
        remote(dst, dst, sf.at[0, 0], recv, mate, c).wait_recv()

    for copy in column_copies(0):
        copy.start()
    bias_swap.start()
    send_gather(0)

    for form, w in enumerate((ws, we)):
        wvt[form] = w[:, 2 * channels : 3 * channels].astype(F32).T.astype(BF16)
        wgt[form] = w[:, 3 * channels : 4 * channels].astype(F32).T.astype(BF16)

    relay(0)
    for copy in column_copies(1):
        copy.start()

    def mask_row(t):
        return tm[pl.ds(t, 1), :].astype(F32)

    def penalty(t):
        return (mask_row(t) - 1.0) * 1e9

    for g in range(2):
        row_bias = penalty(2 * c + g)
        for h in range(heads):
            part = (bs[h, :, g * tile : (g + 1) * tile].astype(F32) + row_bias) * LOG2E
            bias[0, h, g * tile : (g + 1) * tile, :] = part.T

    def near_0(u, carry):
        send_near(0, u)
        return carry

    lax.fori_loop(0, nc, near_0, 0)
    relay(1)
    send_gather(1)

    bias_swap.wait_recv()
    for part_ref, rows, t in (
        (be.at[:, :, mine], mine, r),
        (be_in, other, mate),
    ):
        column = jnp.broadcast_to(penalty(t), (tile, tile)).T
        for h in range(heads):
            bias[1, h, rows, :] = (part_ref[h].astype(F32) + column) * LOG2E

    scale = depth ** (-0.5) * LOG2E
    lane = lax.broadcasted_iota(jnp.int32, (tile, channels), 1) // depth
    ones = jnp.ones((16, 2 * tile), BF16)

    def attend(form, w, a):
        rows = kv[form, a]
        keys = nn(rows, w[:, channels : 2 * channels]).astype(BF16)
        values = nt(wvt[form], rows).astype(BF16)
        query = nn(q[form, a], w[:, :channels]) * scale
        for h in range(heads):
            chosen = jnp.where(lane == h, query, 0.0).astype(BF16)
            scores = nt(keys, chosen) + bias[form, h]
            peak = jnp.max(scores, axis=0, keepdims=True)
            probs = jnp.exp2(scores - peak).astype(BF16)
            lhs = jnp.concatenate([values[h * depth : (h + 1) * depth], ones], axis=0)
            total = nn(lhs, probs)
            pn[form, a, h * depth : (h + 1) * depth, :] = total[:depth].astype(BF16)
            pst[form, a, h : h + 1, :] = peak
            pst[form, a, heads + h : heads + h + 1, :] = total[depth : depth + 1]

    own_sem = (rg, rn)
    far_sem = (rn, rg)

    def forward(form, a):
        piece = kv.at[form, a, mine]
        landed(piece, own_sem[form].at[form, a])
        remote(piece, piece, sf.at[form, a], rf.at[form, a], mate, c).start()

    def partial_copies(form, a):
        src_n, src_s = pn.at[form, a], pst.at[form, a]
        sems = (spn.at[form, a], sps.at[form, a])
        if form == 0:
            to, b = a // per, lax.rem(a, per)
            return (
                to == c, r, to,
                (src_n, rsn.at[c, b], sems[0], rsn_sem.at[c, b]),
                (src_s, rss.at[c, b], sems[1], rss_sem.at[c, b]),
            )
        return (
            a == r, a, c,
            (src_n, ren.at[r], sems[0], ren_sem.at[r]),
            (src_s, res.at[r], sems[1], res_sem.at[r]),
        )

    def run_form(form, w):
        look = LOOK if form == 0 else n

        def ahead(t, carry):
            forward(form, turn(t))
            return carry

        lax.fori_loop(0, look, ahead, 0)

        def step(t, carry):
            a = turn(t)
            if form == 0:
                @pl.when(t < nc)
                def _():
                    send_near(1, t)
            if look < n:
                @pl.when(t + look < n)
                def _():
                    forward(form, turn(t + look))
            landed(q.at[form, a], far_sem[form].at[form, a])
            landed(kv.at[form, a, other], rf.at[form, a])
            attend(form, w, a)
            here, row, col, numer, stats = partial_copies(form, a)
            either(here, *numer, row, col)
            either(here, *stats, row, col)
            return carry

        lax.fori_loop(0, n, step, 0)

    def combine(parts, stats):
        peaks = [s[:heads] for s in stats]
        largest = functools.reduce(jnp.maximum, peaks)
        factors = [jnp.exp2(p - largest) for p in peaks]
        denom = sum(f * s[heads:] for f, s in zip(factors, stats))
        rows = []
        for h in range(heads):
            pick = slice(h * depth, (h + 1) * depth)
            total = sum(f[h : h + 1] * p[pick].astype(F32) for f, p in zip(factors, parts))
            rows.append(total / denom[h : h + 1])
        return jnp.concatenate(rows, axis=0)

    def finish(form, attended, rows, weight, mask):
        gate = nt(wgt[form], rows)
        gated = jax.nn.sigmoid(gate) * attended * mask
        return nn(gated.T.astype(BF16), weight).astype(BF16)

    run_form(0, ws)
    run_form(1, we)

    for b in range(per):
        a = per * c + b
        for g in range(nc):
            landed(rsn.at[g, b], rsn_sem.at[g, b])
            landed(rss.at[g, b], rss_sem.at[g, b])
        attended = combine([rsn[g, b] for g in range(nc)], [rss[g, b] for g in range(nc)])
        mask = mask_row(r) * tms[offs[0] + a].astype(F32)
        out_s[b] = finish(0, attended, q[0, a], wso[...], mask)

    for e in range(2):
        for m in range(nc):
            landed(ren.at[2 * m + e], ren_sem.at[2 * m + e])
            landed(res.at[2 * m + e], res_sem.at[2 * m + e])
        attended = combine(
            [ren[2 * m + e] for m in range(nc)], [res[2 * m + e] for m in range(nc)]
        )
        mask = mask_row(2 * c + e) * tms[offs[1] + r].astype(F32)
        rows = cols[1, c, e * tile : (e + 1) * tile, :]
        out_e[0, e * tile : (e + 1) * tile, :] = finish(1, attended, rows, weo[...], mask)

    bias_swap.wait_send()
    for form in range(2):
        drain_form(form)

        def drain(a, carry):
            piece = kv.at[form, a, mine]
            remote(piece, piece, sf.at[form, a], rf.at[form, a], mate, c).wait_send()
            here, _, _, numer, stats = partial_copies(form, a)
            sent(here, *numer)
            sent(here, *stats)
            return carry

        lax.fori_loop(0, n, drain, 0)


def local(z_rows, z_cols, bias_start, bias_end, w_start_in, w_start_out, w_end_in, w_end_out, token_mask, offsets):
    n, nc = lax.axis_size("row"), lax.axis_size("col")
    heads, tile, span = bias_start.shape
    channels = z_rows.shape[2]
    per = n // nc
    vmem = pl.BlockSpec(memory_space=pltpu.VMEM)
    smem = pl.BlockSpec(memory_space=pltpu.SMEM)
    dma = pltpu.SemaphoreType.DMA
    return pl.pallas_call(
        functools.partial(kernel, n, nc, heads),
        out_shape=(
            jax.ShapeDtypeStruct((per, tile, channels), BF16),
            jax.ShapeDtypeStruct((1, span, channels), BF16),
        ),
        in_specs=[vmem] * 9 + [smem] * 2,
        out_specs=(vmem, vmem),
        scratch_shapes=[
            pltpu.VMEM((2, nc, span, channels), BF16),
            pltpu.VMEM((2, n, span, channels), BF16),
            pltpu.VMEM((2, n, tile, channels), BF16),
            pltpu.VMEM((2, heads, span, tile), F32),
            pltpu.VMEM((2, channels, channels), BF16),
            pltpu.VMEM((2, channels, channels), BF16),
            pltpu.VMEM((heads, tile, tile), BF16),
            pltpu.VMEM((2, n, channels, tile), BF16),
            pltpu.VMEM((2, n, 2 * heads, tile), F32),
            pltpu.VMEM((nc, per, channels, tile), BF16),
            pltpu.VMEM((nc, per, 2 * heads, tile), F32),
            pltpu.VMEM((n, channels, tile), BF16),
            pltpu.VMEM((n, 2 * heads, tile), F32),
            dma((2, n)), dma((2, n)), dma((2, nc)), dma((2, nc)), dma((2, n)), dma((2, n)), dma((2, n)), dma,
            dma((2, n)), dma((2, n)), dma((2, nc)), dma((2, n)),
            dma((nc, per)), dma((nc, per)), dma((n,)), dma((n,)), dma,
        ],
        compiler_params=pltpu.CompilerParams(
            collective_id=0, has_side_effects=True, vmem_limit_bytes=32 * 1024 * 1024
        ),
        name="triangle_attention",
    )(
        z_rows, z_cols, bias_start, bias_end, w_start_in, w_start_out, w_end_in, w_end_out,
        token_mask.reshape(-1, tile), token_mask, offsets,
    )


def solution(mesh):
    return jax.shard_map(
        local,
        mesh=mesh,
        in_specs=(
            P("row", "col", None),
            P("row", "col", None),
            P(None, "row", "col"),
            P(None, "row", "col"),
            P(),
            P(),
            P(),
            P(),
            P(),
            P(),
        ),
        out_specs=(P("col", "row", None), P("row", "col", None)),
        check_vma=False,
    )
```

```python
import functools
import math

import jax
import jax.numpy as jnp
from jax import lax
from jax.experimental import pallas as pl
from jax.experimental.pallas import tpu as pltpu
from jax.sharding import PartitionSpec as P

MESH = pl.DeviceIdType.MESH
LOG2E = math.log2(math.e)
BATCH = 4
F32 = jnp.float32
BF16 = jnp.bfloat16


def nn(a, b):
    return lax.dot_general(a, b, (((1,), (0,)), ((), ())), preferred_element_type=F32)


def nt(a, b):
    return lax.dot_general(a, b, (((1,), (1,)), ((), ())), preferred_element_type=F32)


def normalize(block):
    values = block.astype(F32)
    center = values - jnp.mean(values, axis=-1, keepdims=True)
    spread = jnp.mean(center * center, axis=-1, keepdims=True)
    return (center * lax.rsqrt(spread + 1e-05)).astype(BF16)


def kernel(
    n, nc, heads,
    zr_in, zc_in, bs_in, be_far, ws_in, wso_in, we_in, weo_in, tm_in, tms, offs,
    out_s, out_e,
    zr, zc, bs, be, ws, wso, we, weo, tm, got,
    cols, kv, q, bias, wgt, be_in, pn, pst, rsn, rss, ren, res,
    sg, sn, sc, sz, sf, spn, sps, sb,
    rg, rn, rc, rf, rsn_sem, rss_sem, ren_sem, res_sem, rb,
):
    r = lax.axis_index("row")
    c = lax.axis_index("col")
    core = lax.rem(r, 2)
    chip = r // 2
    mate = r + 1 - 2 * core
    tile = tm.shape[1]
    channels = zr.shape[2]
    batch = min(BATCH, n)
    depth = channels // heads
    per = n // nc
    mine = pl.ds(pl.multiple_of(core * tile, tile), tile)
    other = pl.ds(pl.multiple_of((1 - core) * tile, tile), tile)
    deep = nc // 2
    lap, lane_z = c // deep, lax.rem(c, deep)
    twin = (1 - lap) * deep + lane_z

    def level(d):
        return lap * deep + lax.rem(lane_z + d, deep)

    def turn(t):
        return 2 * lax.rem(chip + nc - t // 2, nc) + lax.rem(t, 2)

    fetches = [
        pltpu.make_async_copy(src, dst, got.at[k])
        for k, (src, dst) in enumerate((
            (zr_in, zr), (zc_in, zc), (ws_in, ws), (we_in, we), (tm_in, tm), (bs_in, bs),
            (be_far.at[:, :, mine], be), (wso_in, wso), (weo_in, weo),
        ))
    ]
    for fetch in fetches:
        fetch.start()

    barrier = pltpu.get_barrier_semaphore()

    def greet(row, col):
        pl.semaphore_signal(barrier, inc=1, device_id=(row, col), device_id_type=MESH)

    def greet_row(d, carry):
        greet(lax.rem(r + d, n), c)
        return carry

    def greet_col(d, carry):
        greet(r, lax.rem(c + d, nc))
        return carry

    lax.fori_loop(1, n, greet_row, 0)
    lax.fori_loop(1, nc, greet_col, 0)

    fetches[0].wait()
    cols[0, c] = normalize(zr[0])
    fetches[1].wait()
    cols[1, c] = normalize(zc[0])

    pl.semaphore_wait(barrier, n - 1 + nc - 1)

    def half(form, block, e):
        return cols.at[form, block, pl.ds(e * tile, tile)]

    def gather_copy(form, to, e):
        if form == 0:
            dst = kv.at[0, r, pl.ds(e * tile, tile)]
        else:
            dst = q.at[1, r]
        return half(form, c, e), dst, sg.at[form, 2 * to + e], rg.at[form, r]

    def near_copy(form, to, e):
        if form == 0:
            dst = q.at[0, r]
        else:
            dst = kv.at[1, r, pl.ds(e * tile, tile)]
        return half(form, to, e), dst, sn.at[form, 2 * to + e], rn.at[form, r]

    def remote(src, dst, send, recv, row, col):
        return pltpu.make_async_remote_copy(
            src_ref=src, dst_ref=dst, send_sem=send, recv_sem=recv,
            device_id=(row, col), device_id_type=MESH,
        )

    def either(here, src, dst, send, recv, row, col):
        @pl.when(here)
        def _():
            pltpu.make_async_copy(src, dst, recv).start()
        @pl.when(jnp.logical_not(here))
        def _():
            remote(src, dst, send, recv, row, col).start()

    def sent(here, src, dst, send, recv):
        @pl.when(jnp.logical_not(here))
        def _():
            remote(src, dst, send, recv, mate, c).wait_send()

    bias_swap = remote(
        be_far.at[:, :, other], be_in, sb, rb, mate, c
    )

    def along(u):
        return lax.rem(chip + u, nc)

    def column_copies(form):
        mine_out = [(twin, sc.at[form, 0])] + [(level(d), sc.at[form, d]) for d in range(1, deep)]
        own = cols.at[form, c]
        return [remote(own, own, sem, rc.at[form, c], r, to) for to, sem in mine_out]

    def relay_copies(form):
        other_block = cols.at[form, twin]
        return [
            remote(other_block, other_block, sz.at[form, d], rc.at[form, twin], r, level(d))
            for d in range(1, deep)
        ]

    def relay(form):
        landed(cols.at[form, twin], rc.at[form, twin])
        for copy in relay_copies(form):
            copy.start()

    def send_gather(form):
        def step(u, carry):
            to = along(u)
            for e in range(2):
                either((u == 0) & (core == e), *gather_copy(form, to, e), 2 * to + e, c)
            return carry
        lax.fori_loop(0, nc, step, 0)

    def send_near(form, u):
        to = along(u)
        @pl.when((to != c) & (to != twin))
        def _():
            landed(cols.at[form, to], rc.at[form, to])
        for e in range(2):
            either((u == 0) & (core == e), *near_copy(form, to, e), 2 * to + e, c)

    def drain_form(form):
        for copy in column_copies(form) + relay_copies(form):
            copy.wait_send()
        def step(u, carry):
            to = along(u)
            for e in range(2):
                here = (u == 0) & (core == e)
                sent(here, *gather_copy(form, to, e))
                sent(here, *near_copy(form, to, e))
            return carry
        lax.fori_loop(0, nc, step, 0)

    def landed(dst, recv):
        remote(dst, dst, sf.at[0, 0], recv, mate, c).wait_recv()

    for copy in column_copies(0):
        copy.start()
    bias_swap.start()
    send_gather(0)

    for fetch in fetches[2:]:
        fetch.wait()
    for form, w in enumerate((ws, we)):
        wgt[form] = w[:, 3 * channels : 4 * channels].astype(F32).T.astype(BF16)

    relay(0)
    for copy in column_copies(1):
        copy.start()

    def mask_row(t):
        return tm[pl.ds(t, 1), :].astype(F32)

    def penalty(t):
        return (mask_row(t) - 1.0) * 1e9

    key_bias = jnp.concatenate([penalty(2 * c), penalty(2 * c + 1)], axis=1)
    for h in range(heads):
        bias[0, h] = (bs[h].astype(F32) + key_bias) * LOG2E

    def near_0(u, carry):
        send_near(0, u)
        return carry

    lax.fori_loop(0, nc, near_0, 0)
    relay(1)
    send_gather(1)

    bias_swap.wait_recv()
    for part, cols_at, t in ((be, mine, r), (be_in, other, mate)):
        row = penalty(t)
        for h in range(heads):
            bias[1, h, :, cols_at] = (part[h].astype(F32).T + row) * LOG2E

    scale = depth ** (-0.5) * LOG2E
    lane = lax.broadcasted_iota(jnp.int32, (tile, channels), 1)
    head_of = lane // depth
    ones = jnp.ones((2 * tile, channels), BF16)

    def attend(form, w, turns):
        rows = jnp.concatenate([kv[form, a] for a in turns], axis=0)
        both = nn(rows, w[:, channels : 3 * channels]).astype(BF16)
        rows = jnp.concatenate([q[form, a] for a in turns], axis=0)
        queries = nn(rows, w[:, :channels]) * scale
        for i, a in enumerate(turns):
            keys = both[2 * i * tile : 2 * (i + 1) * tile, :channels]
            values = both[2 * i * tile : 2 * (i + 1) * tile, channels:]
            query = queries[i * tile : (i + 1) * tile]
            chosen = [jnp.where(head_of == h, query, 0.0).astype(BF16) for h in range(heads)]
            scores = nt(jnp.concatenate(chosen, axis=0), keys)
            stats = jnp.zeros((tile, channels), F32)
            probs = []
            for h in range(heads):
                part = scores[h * tile : (h + 1) * tile] + bias[form, h]
                peak = jnp.max(part, axis=1, keepdims=True)
                probs.append(jnp.exp2(part - peak).astype(BF16))
                stats = jnp.where(lane == h, peak, stats)
            totals = nn(jnp.concatenate(probs, axis=0), jnp.concatenate([values, ones], axis=1))
            numer = jnp.zeros((tile, channels), F32)
            for h in range(heads):
                part = totals[h * tile : (h + 1) * tile]
                numer = jnp.where(head_of == h, part[:, :channels], numer)
                stats = jnp.where(lane == heads + h, part[:, channels:], stats)
            pn[form, a] = numer.T.astype(BF16)
            pst[form, a] = stats.T[: 2 * heads]

    own_sem = (rg, rn)
    far_sem = (rn, rg)

    def forward(form, a):
        piece = kv.at[form, a, mine]
        landed(piece, own_sem[form].at[form, a])
        remote(piece, piece, sf.at[form, a], rf.at[form, a], mate, c).start()

    def partial_copies(form, a):
        src_n, src_s = pn.at[form, a], pst.at[form, a]
        sems = (spn.at[form, a], sps.at[form, a])
        if form == 0:
            to, b = a // per, lax.rem(a, per)
            return (
                to == c, r, to,
                (src_n, rsn.at[c, b], sems[0], rsn_sem.at[c, b]),
                (src_s, rss.at[c, b], sems[1], rss_sem.at[c, b]),
            )
        return (
            a == r, a, c,
            (src_n, ren.at[r], sems[0], ren_sem.at[r]),
            (src_s, res.at[r], sems[1], res_sem.at[r]),
        )

    def run_form(form, w):
        def ahead(b):
            for k in range(batch):
                forward(form, turn(batch * b + k))

        ahead(0)

        def step(b, carry):
            turns = [turn(batch * b + k) for k in range(batch)]
            if form == 0:
                @pl.when(batch * b < nc)
                def _():
                    for k in range(min(batch, nc)):
                        send_near(1, batch * b + k)
            @pl.when(batch * (b + 1) < n)
            def _():
                ahead(b + 1)
            for a in turns:
                landed(q.at[form, a], far_sem[form].at[form, a])
                landed(kv.at[form, a, other], rf.at[form, a])
            attend(form, w, turns)
            for a in turns:
                here, row, col, numer, stats = partial_copies(form, a)
                either(here, *numer, row, col)
                either(here, *stats, row, col)
            return carry

        lax.fori_loop(0, n // batch, step, 0)

    def combine(parts, stats):
        peaks = [s[:heads] for s in stats]
        largest = functools.reduce(jnp.maximum, peaks)
        factors = [jnp.exp2(p - largest) for p in peaks]
        denom = sum(f * s[heads:] for f, s in zip(factors, stats))
        rows = []
        for h in range(heads):
            pick = slice(h * depth, (h + 1) * depth)
            total = sum(f[h : h + 1] * p[pick].astype(F32) for f, p in zip(factors, parts))
            rows.append(total / denom[h : h + 1])
        return jnp.concatenate(rows, axis=0)

    def finish(form, attended, rows, weight, mask):
        gate = nt(wgt[form], rows)
        gated = jax.nn.sigmoid(gate) * attended * mask
        return nn(gated.T.astype(BF16), weight).astype(BF16)

    run_form(0, ws)
    run_form(1, we)

    for b in range(per):
        a = per * c + b
        for g in range(nc):
            landed(rsn.at[g, b], rsn_sem.at[g, b])
            landed(rss.at[g, b], rss_sem.at[g, b])
        attended = combine([rsn[g, b] for g in range(nc)], [rss[g, b] for g in range(nc)])
        mask = mask_row(r) * tms[offs[0] + a].astype(F32)
        out_s[b] = finish(0, attended, q[0, a], wso[...], mask)

    for e in range(2):
        for m in range(nc):
            landed(ren.at[2 * m + e], ren_sem.at[2 * m + e])
            landed(res.at[2 * m + e], res_sem.at[2 * m + e])
        attended = combine(
            [ren[2 * m + e] for m in range(nc)], [res[2 * m + e] for m in range(nc)]
        )
        mask = mask_row(2 * c + e) * tms[offs[1] + r].astype(F32)
        rows = cols[1, c, e * tile : (e + 1) * tile, :]
        out_e[0, e * tile : (e + 1) * tile, :] = finish(1, attended, rows, weo[...], mask)

    bias_swap.wait_send()
    for form in range(2):
        drain_form(form)

        def drain(a, carry):
            piece = kv.at[form, a, mine]
            remote(piece, piece, sf.at[form, a], rf.at[form, a], mate, c).wait_send()
            here, _, _, numer, stats = partial_copies(form, a)
            sent(here, *numer)
            sent(here, *stats)
            return carry

        lax.fori_loop(0, n, drain, 0)


def local(z_rows, z_cols, bias_start, bias_end, w_start_in, w_start_out, w_end_in, w_end_out, token_mask, offsets):
    n, nc = lax.axis_size("row"), lax.axis_size("col")
    heads, tile, span = bias_start.shape
    channels = z_rows.shape[2]
    per = n // nc
    vmem = pl.BlockSpec(memory_space=pltpu.VMEM)
    smem = pl.BlockSpec(memory_space=pltpu.SMEM)
    dma = pltpu.SemaphoreType.DMA
    return pl.pallas_call(
        functools.partial(kernel, n, nc, heads),
        out_shape=(
            jax.ShapeDtypeStruct((per, tile, channels), BF16),
            jax.ShapeDtypeStruct((1, span, channels), BF16),
        ),
        in_specs=[pl.BlockSpec(memory_space=pl.ANY)] * 9 + [smem] * 2,
        out_specs=(vmem, vmem),
        scratch_shapes=[
            pltpu.VMEM(z_rows.shape, BF16),
            pltpu.VMEM(z_cols.shape, BF16),
            pltpu.VMEM(bias_start.shape, BF16),
            pltpu.VMEM((heads, tile, tile), BF16),
            pltpu.VMEM(w_start_in.shape, BF16),
            pltpu.VMEM(w_start_out.shape, BF16),
            pltpu.VMEM(w_end_in.shape, BF16),
            pltpu.VMEM(w_end_out.shape, BF16),
            pltpu.VMEM((n, tile), jnp.int32),
            dma((9,)),
            pltpu.VMEM((2, nc, span, channels), BF16),
            pltpu.VMEM((2, n, span, channels), BF16),
            pltpu.VMEM((2, n, tile, channels), BF16),
            pltpu.VMEM((2, heads, tile, span), F32),
            pltpu.VMEM((2, channels, channels), BF16),
            pltpu.VMEM((heads, tile, tile), BF16),
            pltpu.VMEM((2, n, channels, tile), BF16),
            pltpu.VMEM((2, n, 2 * heads, tile), F32),
            pltpu.VMEM((nc, per, channels, tile), BF16),
            pltpu.VMEM((nc, per, 2 * heads, tile), F32),
            pltpu.VMEM((n, channels, tile), BF16),
            pltpu.VMEM((n, 2 * heads, tile), F32),
            dma((2, n)), dma((2, n)), dma((2, nc)), dma((2, nc)), dma((2, n)), dma((2, n)), dma((2, n)), dma,
            dma((2, n)), dma((2, n)), dma((2, nc)), dma((2, n)),
            dma((nc, per)), dma((nc, per)), dma((n,)), dma((n,)), dma,
        ],
        compiler_params=pltpu.CompilerParams(
            collective_id=0, has_side_effects=True, vmem_limit_bytes=62 * 1024 * 1024
        ),
        name="triangle_attention",
    )(
        z_rows, z_cols, bias_start, bias_end, w_start_in, w_start_out, w_end_in, w_end_out,
        token_mask.reshape(-1, tile), token_mask, offsets,
    )


def solution(mesh):
    return jax.shard_map(
        local,
        mesh=mesh,
        in_specs=(
            P("row", "col", None),
            P("row", "col", None),
            P(None, "row", "col"),
            P(None, "row", "col"),
            P(),
            P(),
            P(),
            P(),
            P(),
            P(),
        ),
        out_specs=(P("col", "row", None), P("row", "col", None)),
        check_vma=False,
    )
```

```python
import functools
import math

import jax
import jax.numpy as jnp
from jax import lax
from jax.experimental import pallas as pl
from jax.experimental.pallas import tpu as pltpu
from jax.sharding import PartitionSpec as P

MESH = pl.DeviceIdType.MESH
LOG2E = math.log2(math.e)
BATCH = 4
F32 = jnp.float32
BF16 = jnp.bfloat16


def nn(a, b):
    return lax.dot_general(a, b, (((1,), (0,)), ((), ())), preferred_element_type=F32)


def nt(a, b):
    return lax.dot_general(a, b, (((1,), (1,)), ((), ())), preferred_element_type=F32)


def normalize(block):
    values = block.astype(F32)
    center = values - jnp.mean(values, axis=-1, keepdims=True)
    spread = jnp.mean(center * center, axis=-1, keepdims=True)
    return (center * lax.rsqrt(spread + 1e-05)).astype(BF16)


def kernel(
    n, nc, heads,
    zr_in, zc_in, bs_in, be_far, ws_in, wso_in, we_in, weo_in, tm_in, offs,
    out_s, out_e,
    zr, zc, bs, be, ws, wso, we, weo, tm, tms, got,
    x, across, scat, kv, q, bias, wgt, be_in, pn, pst, rsn, rss, ren, res,
    ss, sa, sg, sc, sf, spn, sps, sb,
    rs, ra, rg, ry, rt, rn, rf, rsn_sem, rss_sem, ren_sem, res_sem, rb,
):
    r = lax.axis_index("row")
    c = lax.axis_index("col")
    core = lax.rem(r, 2)
    chip = r // 2
    mate = r + 1 - 2 * core
    tile = tm.shape[1]
    channels = zr.shape[2]
    batch = min(BATCH, n)
    depth = channels // heads
    per = n // nc
    mine = pl.ds(pl.multiple_of(core * tile, tile), tile)
    other = pl.ds(pl.multiple_of((1 - core) * tile, tile), tile)
    deep = nc // 2
    lap, lane_z = c // deep, lax.rem(c, deep)
    twin = (1 - lap) * deep + lane_z

    def level(d):
        return lap * deep + lax.rem(lane_z + d, deep)

    groups = n // batch
    piece = tile // nc
    block = chip // 2
    facing = r + 2 - 4 * lax.rem(chip, 2)

    def group(b):
        return lax.rem(block + groups - b, groups)

    def along(u):
        return 2 * lax.rem(block + u // 2, groups) + lax.rem(chip + u, 2)

    def part(p):
        return pl.ds(pl.multiple_of(p * piece, piece), piece)

    fetches = [
        pltpu.make_async_copy(src, dst, got.at[k])
        for k, (src, dst) in enumerate((
            (zr_in, zr), (zc_in, zc), (ws_in, ws), (we_in, we), (tm_in, tm), (bs_in, bs),
            (be_far.at[:, :, mine], be), (wso_in, wso), (weo_in, weo), (tm_in, tms),
        ))
    ]
    for fetch in fetches:
        fetch.start()

    barrier = pltpu.get_barrier_semaphore()

    def greet(row, col):
        pl.semaphore_signal(barrier, inc=1, device_id=(row, col), device_id_type=MESH)

    def greet_row(d, carry):
        greet(lax.rem(r + d, n), c)
        return carry

    def greet_col(d, carry):
        greet(r, lax.rem(c + d, nc))
        return carry

    lax.fori_loop(1, n, greet_row, 0)
    lax.fori_loop(1, nc, greet_col, 0)

    fetches[0].wait()
    x[0] = normalize(zr[0]).reshape(2, tile, channels)
    fetches[1].wait()
    x[1] = normalize(zc[0]).reshape(2, tile, channels)
    for form in range(2):
        for e in range(2):
            scat[c, form, e] = x[form, e, part(c), :]

    for fetch in fetches[2:]:
        fetch.wait()
    for form, w in enumerate((ws, we)):
        wgt[form] = w[:, 3 * channels : 4 * channels].astype(F32).T.astype(BF16)

    def mask_row(t):
        return tm[pl.ds(t, 1), :].astype(F32)

    def penalty(t):
        return (mask_row(t) - 1.0) * 1e9

    key_bias = jnp.concatenate([penalty(2 * c), penalty(2 * c + 1)], axis=1)
    for h in range(heads):
        bias[0, h] = (bs[h].astype(F32) + key_bias) * LOG2E

    pl.semaphore_wait(barrier, n - 1 + nc - 1)

    def remote(src, dst, send, recv, row, col):
        return pltpu.make_async_remote_copy(
            src_ref=src, dst_ref=dst, send_sem=send, recv_sem=recv,
            device_id=(row, col), device_id_type=MESH,
        )

    def either(here, src, dst, send, recv, row, col):
        @pl.when(here)
        def _():
            pltpu.make_async_copy(src, dst, recv).start()
        @pl.when(jnp.logical_not(here))
        def _():
            remote(src, dst, send, recv, row, col).start()

    bias_swap = remote(
        be_far.at[:, :, other], be_in, sb, rb, mate, c
    )

    def landed(dst, recv):
        remote(dst, dst, sb, recv, mate, c).wait_recv()

    def gone(src, send):
        remote(src, src, send, rb, mate, c).wait_send()

    def scatter(d, carry):
        to = lax.rem(c + d, nc)
        remote(x.at[:, :, part(to)], scat.at[c], ss, rs, r, to).start()
        return carry

    def cross(form):
        def step(u, carry):
            to = along(u)
            for e in range(2):
                dst = q.at[0, r, part(c)] if form == 0 else kv.at[1, r, e, part(c)]
                src = scat.at[to, form, e]
                either((u == 0) & (core == e), src, dst, sa.at[form], ra.at[form, block], 2 * to + e, c)
            return carry
        lax.fori_loop(0, nc, step, 0)

    def near_piece(form, g, p):
        rows = pl.ds(batch * g, batch)
        return q.at[0, rows, part(p)] if form == 0 else kv.at[1, rows, core, part(p)]

    def near_twin(form, b):
        g = group(b)
        landed(q.at[0, pl.ds(0, batch), part(0)], ra.at[form, g])
        own = near_piece(form, g, c)
        remote(own, own, sc.at[form], rt.at[form, g], r, twin).start()

    def near_levels(form, b, held):
        g = group(b)
        piece_ref = near_piece(form, g, held)
        for d in range(1, deep):
            remote(piece_ref, piece_ref, sc.at[form], rn.at[form, g], r, level(d)).start()

    def relay(form, b):
        landed(near_piece(form, group(b), twin), rt.at[form, group(b)])
        near_levels(form, b, twin)

    def send_facing(form):
        remote(x.at[form], across.at[form], sg.at[form], ry.at[form], facing, c).start()

    def spread(form, held, row):
        for k in range(groups):
            to = 4 * lax.rem(block + k, groups) + 2 * lax.rem(chip, 2)
            for e in range(2):
                dst = kv.at[0, row, e] if form == 0 else q.at[1, row]
                recv = rg.at[form, block]
                if k == 0:
                    either(core == e, held.at[form, e], dst, sg.at[form], recv, to + e, c)
                else:
                    remote(held.at[form, e], dst, sg.at[form], recv, to + e, c).start()

    def spread_facing(form):
        landed(x.at[form], ry.at[form])
        spread(form, across, facing)

    lax.fori_loop(1, nc, scatter, 0)
    send_facing(0)
    spread(0, x, r)
    landed(scat.at[pl.ds(0, nc - 1)], rs)
    cross(0)
    spread_facing(0)
    cross(1)
    bias_swap.start()
    send_facing(1)

    for b in range(groups):
        near_twin(0, b)
    for b in range(groups):
        near_levels(0, b, c)
        if b:
            relay(0, b - 1)
    relay(0, groups - 1)
    spread(1, x, r)
    for b in range(groups):
        near_twin(1, b)
    for b in range(groups):
        near_levels(1, b, c)

    bias_swap.wait_recv()
    for source, cols_at, t in ((be, mine, r), (be_in, other, mate)):
        row = penalty(t)
        for h in range(heads):
            bias[1, h, :, cols_at] = (source[h].astype(F32).T + row) * LOG2E

    scale = depth ** (-0.5) * LOG2E
    lane = lax.broadcasted_iota(jnp.int32, (tile, channels), 1)
    head_of = lane // depth
    ones = jnp.ones((2 * tile, channels), BF16)

    def attend(form, w, g):
        held = pl.ds(batch * g, batch)
        rows = kv[form, held].reshape(2 * batch * tile, channels)
        both = nn(rows, w[:, channels : 3 * channels]).astype(BF16)
        rows = q[form, held].reshape(batch * tile, channels)
        queries = nn(rows, w[:, :channels]) * scale
        for i in range(batch):
            a = batch * g + i
            keys = both[2 * i * tile : 2 * (i + 1) * tile, :channels]
            values = both[2 * i * tile : 2 * (i + 1) * tile, channels:]
            query = queries[i * tile : (i + 1) * tile]
            chosen = [jnp.where(head_of == h, query, 0.0).astype(BF16) for h in range(heads)]
            scores = nt(jnp.concatenate(chosen, axis=0), keys)
            stats = jnp.zeros((tile, channels), F32)
            probs = []
            for h in range(heads):
                part = scores[h * tile : (h + 1) * tile] + bias[form, h]
                peak = jnp.max(part, axis=1, keepdims=True)
                probs.append(jnp.exp2(part - peak).astype(BF16))
                stats = jnp.where(lane == h, peak, stats)
            totals = nn(jnp.concatenate(probs, axis=0), jnp.concatenate([values, ones], axis=1))
            numer = jnp.zeros((tile, channels), F32)
            for h in range(heads):
                part = totals[h * tile : (h + 1) * tile]
                numer = jnp.where(head_of == h, part[:, :channels], numer)
                stats = jnp.where(lane == heads + h, part[:, channels:], stats)
            pn[form, a] = numer.T.astype(BF16)
            pst[form, a] = stats.T[: 2 * heads]

    def forward_copy(form, g):
        held = kv.at[form, pl.ds(batch * g, batch), core]
        return remote(held, held, sf.at[form], rf.at[form, g], mate, c)

    def near_landed(form, g):
        if deep > 1:
            landed(q.at[0, pl.ds(0, (nc - 2) * batch // nc)], rn.at[form, g])

    def gather_landed(form, g):
        landed(q.at[0, pl.ds(0, batch)], rg.at[form, g])

    def forward(form, b):
        (gather_landed if form == 0 else near_landed)(form, group(b))
        forward_copy(form, group(b)).start()

    def send_partial(form, a):
        if form == 0:
            to, b = a // per, lax.rem(a, per)
            pairs = (rsn.at[c, b], rsn_sem), (rss.at[c, b], rss_sem)
            here, row, col = to == c, r, to
        else:
            pairs = (ren.at[core, chip], ren_sem.at[core]), (res.at[core, chip], res_sem.at[core])
            here, row, col = a == r, a, c
        either(here, pn.at[form, a], pairs[0][0], spn.at[form], pairs[0][1], row, col)
        either(here, pst.at[form, a], pairs[1][0], sps.at[form], pairs[1][1], row, col)

    def run_form(form, w):
        forward(form, 0)

        def step(b, carry):
            g = group(b)
            if form == 0:
                @pl.when(b == 0)
                def _():
                    spread_facing(1)
                relay(1, b)
            @pl.when(b + 1 < groups)
            def _():
                forward(form, b + 1)
            (near_landed if form == 0 else gather_landed)(form, g)
            forward_copy(form, g).wait_recv()
            if form == 1:
                for k in range(batch):
                    send_partial(0, batch * g + k)
            attend(form, w, g)
            if form == 1:
                for k in range(batch):
                    send_partial(1, batch * g + k)
            return carry

        lax.fori_loop(0, groups, step, 0)

    def combine(parts, stats):
        peaks = [s[:heads] for s in stats]
        largest = functools.reduce(jnp.maximum, peaks)
        factors = [jnp.exp2(p - largest) for p in peaks]
        denom = sum(f * s[heads:] for f, s in zip(factors, stats))
        rows = []
        for h in range(heads):
            pick = slice(h * depth, (h + 1) * depth)
            total = sum(f[h : h + 1] * p[pick].astype(F32) for f, p in zip(factors, parts))
            rows.append(total / denom[h : h + 1])
        return jnp.concatenate(rows, axis=0)

    def finish(form, attended, rows, weight, mask):
        gate = nt(wgt[form], rows)
        gated = jax.nn.sigmoid(gate) * attended * mask
        return nn(gated.T.astype(BF16), weight).astype(BF16)

    run_form(0, ws)
    run_form(1, we)

    def mask_scalar(k, a):
        at = offs[k] + a
        return tms[at // tile, lax.rem(at, tile)].astype(F32)

    landed(rsn, rsn_sem)
    landed(rss, rss_sem)
    for b in range(per):
        a = per * c + b
        attended = combine([rsn[g, b] for g in range(nc)], [rss[g, b] for g in range(nc)])
        mask = mask_row(r) * mask_scalar(0, a)
        out_s[b] = finish(0, attended, q[0, a], wso[...], mask)

    for e in range(2):
        landed(ren.at[e], ren_sem.at[e])
        landed(res.at[e], res_sem.at[e])
        attended = combine([ren[e, m] for m in range(nc)], [res[e, m] for m in range(nc)])
        mask = mask_row(2 * c + e) * mask_scalar(1, r)
        out_e[0, e * tile : (e + 1) * tile, :] = finish(1, attended, x[1, e], weo[...], mask)

    bias_swap.wait_send()
    gone(scat.at[pl.ds(0, nc - 1)], ss)
    for form in range(2):
        gone(q.at[0, pl.ds(0, n - 1), part(0)], sa.at[form])
        gone(q.at[0], sg.at[form])
        gone(q.at[0, pl.ds(0, (nc - 1) * per)], sc.at[form])
        gone(q.at[0], sf.at[form])
        remote_count = n - per if form == 0 else n - 1
        gone(pn.at[form, pl.ds(0, remote_count)], spn.at[form])
        gone(pst.at[form, pl.ds(0, remote_count)], sps.at[form])


def local(z_rows, z_cols, bias_start, bias_end, w_start_in, w_start_out, w_end_in, w_end_out, token_mask, offsets):
    n, nc = lax.axis_size("row"), lax.axis_size("col")
    heads, tile, span = bias_start.shape
    channels = z_rows.shape[2]
    per = n // nc
    groups = n // min(BATCH, n)
    vmem = pl.BlockSpec(memory_space=pltpu.VMEM)
    smem = pl.BlockSpec(memory_space=pltpu.SMEM)
    dma = pltpu.SemaphoreType.DMA
    return pl.pallas_call(
        functools.partial(kernel, n, nc, heads),
        out_shape=(
            jax.ShapeDtypeStruct((per, tile, channels), BF16),
            jax.ShapeDtypeStruct((1, span, channels), BF16),
        ),
        in_specs=[pl.BlockSpec(memory_space=pl.ANY)] * 9 + [smem],
        out_specs=(vmem, vmem),
        scratch_shapes=[
            pltpu.VMEM(z_rows.shape, BF16),
            pltpu.VMEM(z_cols.shape, BF16),
            pltpu.VMEM(bias_start.shape, BF16),
            pltpu.VMEM((heads, tile, tile), BF16),
            pltpu.VMEM(w_start_in.shape, BF16),
            pltpu.VMEM(w_start_out.shape, BF16),
            pltpu.VMEM(w_end_in.shape, BF16),
            pltpu.VMEM(w_end_out.shape, BF16),
            pltpu.VMEM((n, tile), jnp.int32),
            pltpu.SMEM((n, tile), jnp.int32),
            dma((10,)),
            pltpu.VMEM((2, 2, tile, channels), BF16),
            pltpu.VMEM((2, 2, tile, channels), BF16),
            pltpu.VMEM((nc, 2, 2, tile // nc, channels), BF16),
            pltpu.VMEM((2, n, 2, tile, channels), BF16),
            pltpu.VMEM((2, n, tile, channels), BF16),
            pltpu.VMEM((2, heads, tile, span), F32),
            pltpu.VMEM((2, channels, channels), BF16),
            pltpu.VMEM((heads, tile, tile), BF16),
            pltpu.VMEM((2, n, channels, tile), BF16),
            pltpu.VMEM((2, n, 2 * heads, tile), F32),
            pltpu.VMEM((nc, per, channels, tile), BF16),
            pltpu.VMEM((nc, per, 2 * heads, tile), F32),
            pltpu.VMEM((2, nc, channels, tile), BF16),
            pltpu.VMEM((2, nc, 2 * heads, tile), F32),
            dma, dma((2,)), dma((2,)), dma((2,)), dma((2,)), dma((2,)), dma((2,)), dma,
            dma, dma((2, groups)), dma((2, groups)), dma((2,)), dma((2, groups)), dma((2, groups)), dma((2, groups)),
            dma, dma, dma((2,)), dma((2,)), dma,
        ],
        compiler_params=pltpu.CompilerParams(
            collective_id=0, has_side_effects=True, vmem_limit_bytes=62 * 1024 * 1024
        ),
        name="triangle_attention",
    )(
        z_rows, z_cols, bias_start, bias_end, w_start_in, w_start_out, w_end_in, w_end_out,
        token_mask.reshape(-1, tile), offsets,
    )


def solution(mesh):
    return jax.shard_map(
        local,
        mesh=mesh,
        in_specs=(
            P("row", "col", None),
            P("row", "col", None),
            P(None, "row", "col"),
            P(None, "row", "col"),
            P(),
            P(),
            P(),
            P(),
            P(),
            P(),
        ),
        out_specs=(P("col", "row", None), P("row", "col", None)),
        check_vma=False,
    )
```

```python
import functools
import math

import jax
import jax.numpy as jnp
from jax import lax
from jax.experimental import pallas as pl
from jax.experimental.pallas import tpu as pltpu
from jax.sharding import PartitionSpec as P

MESH = pl.DeviceIdType.MESH
LOG2E = math.log2(math.e)
BATCH = 4
MERGE = 2
F32 = jnp.float32
BF16 = jnp.bfloat16


def nn(a, b):
    return lax.dot_general(a, b, (((1,), (0,)), ((), ())), preferred_element_type=F32)


def nt(a, b):
    return lax.dot_general(a, b, (((1,), (1,)), ((), ())), preferred_element_type=F32)


def normalize(block):
    values = block.astype(F32)
    center = values - jnp.mean(values, axis=-1, keepdims=True)
    spread = jnp.mean(center * center, axis=-1, keepdims=True)
    return (center * lax.rsqrt(spread + 1e-05)).astype(BF16)


def kernel(
    n, nc, heads,
    zr_in, zc_in, bs_in, be_far, ws_in, wso_in, we_in, weo_in, tm_in, offs,
    out_s, out_e,
    zr, zc, bs, be, ws, wso, we, weo, tm, tms, got,
    x, across, scat, kv, q, bias, wgt, be_in, pn, pst, rsn, rss, ren, res, twn, tws, projected,
    ss, sa, sg, sc, sf, spn, sps, sb,
    rs, ra, rg, ry, rt, rn, rf, rsn_sem, rss_sem, ren_sem, res_sem, twn_sem, tws_sem, rb,
):
    r = lax.axis_index("row")
    c = lax.axis_index("col")
    core = lax.rem(r, 2)
    chip = r // 2
    mate = r + 1 - 2 * core
    tile = tm.shape[1]
    channels = zr.shape[2]
    batch = min(BATCH, n)
    depth = channels // heads
    per = n // nc
    mine = pl.ds(pl.multiple_of(core * tile, tile), tile)
    other = pl.ds(pl.multiple_of((1 - core) * tile, tile), tile)
    deep = nc // 2
    lap, lane_z = c // deep, lax.rem(c, deep)
    twin = (1 - lap) * deep + lane_z

    def level(d):
        return lap * deep + lax.rem(lane_z + d, deep)

    groups = n // batch
    piece = tile // nc
    block = chip // 2
    facing = r + 2 - 4 * lax.rem(chip, 2)

    side = groups // 2
    spans = [3, 1, 2, 0] if groups == 4 else [k % groups for k in range(1, groups + 1)]

    def group(form, b):
        if form == 0:
            return lax.rem(block + groups - b, groups)
        span = spans[0]
        for k in range(1, groups):
            span = jnp.where(b == k, spans[k], span)
        return lax.rem(block + groups - span, groups)

    def along(u):
        return 2 * lax.rem(block + u // 2, groups) + lax.rem(chip + u, 2)

    def mask_row(t):
        return tm[pl.ds(t, 1), :].astype(F32)

    def penalty(t):
        return (mask_row(t) - 1.0) * 1e9

    def part(p):
        return pl.ds(pl.multiple_of(p * piece, piece), piece)

    fetches = [
        pltpu.make_async_copy(src, dst, got.at[k])
        for k, (src, dst) in enumerate((
            (zr_in, zr), (zc_in, zc), (ws_in, ws), (we_in, we), (tm_in, tm), (bs_in, bs),
            (be_far.at[:, :, mine], be), (wso_in, wso), (weo_in, weo), (tm_in, tms),
        ))
    ]
    for fetch in fetches[:2]:
        fetch.start()

    barrier = pltpu.get_barrier_semaphore()

    def greet(row, col):
        pl.semaphore_signal(barrier, inc=1, device_id=(row, col), device_id_type=MESH)

    def greet_row(d, carry):
        greet(lax.rem(r + d, n), c)
        return carry

    def greet_col(d, carry):
        greet(r, lax.rem(c + d, nc))
        return carry

    lax.fori_loop(1, n, greet_row, 0)
    lax.fori_loop(1, nc, greet_col, 0)

    for fetch in fetches[2:]:
        fetch.start()

    fetches[0].wait()
    x[0] = normalize(zr[0]).reshape(2, tile, channels)
    fetches[1].wait()
    x[1] = normalize(zc[0]).reshape(2, tile, channels)
    for form in range(2):
        for e in range(2):
            scat[c, form, e] = x[form, e, part(c), :]

    pl.semaphore_wait(barrier, n - 1 + nc - 1)

    def remote(src, dst, send, recv, row, col):
        return pltpu.make_async_remote_copy(
            src_ref=src, dst_ref=dst, send_sem=send, recv_sem=recv,
            device_id=(row, col), device_id_type=MESH,
        )

    def either(here, src, dst, send, recv, row, col):
        @pl.when(here)
        def _():
            pltpu.make_async_copy(src, dst, recv).start()
        @pl.when(jnp.logical_not(here))
        def _():
            remote(src, dst, send, recv, row, col).start()

    bias_swap = remote(
        be_far.at[:, :, other], be_in, sb, rb, mate, c
    )

    def landed(dst, recv):
        remote(dst, dst, sb, recv, mate, c).wait_recv()

    def gone(src, send):
        remote(src, src, send, rb, mate, c).wait_send()

    def scatter(d, carry):
        to = lax.rem(c + d, nc)
        remote(x.at[:, :, part(to)], scat.at[c], ss, rs, r, to).start()
        return carry

    def cross(form):
        def step(u, carry):
            to = along(u)
            for e in range(2):
                dst = q.at[0, r, part(c)] if form == 0 else kv.at[1, r, e, part(c)]
                src = scat.at[to, form, e]
                either((u == 0) & (core == e), src, dst, sa.at[form], ra.at[form, block], 2 * to + e, c)
            return carry
        lax.fori_loop(0, nc, step, 0)

    def near_piece(form, g, p):
        rows = pl.ds(batch * g, batch)
        return q.at[0, rows, part(p)] if form == 0 else kv.at[1, rows, core, part(p)]

    def near_twin(form, b):
        g = group(form, b)
        landed(q.at[0, pl.ds(0, batch), part(0)], ra.at[form, g])
        own = near_piece(form, g, c)
        remote(own, own, sc.at[form], rt.at[form, g], r, twin).start()

    def near_levels(form, b, held):
        g = group(form, b)
        piece_ref = near_piece(form, g, held)
        for d in range(1, deep):
            remote(piece_ref, piece_ref, sc.at[form], rn.at[form, g], r, level(d)).start()

    def relay(form, b):
        landed(near_piece(form, group(form, b), twin), rt.at[form, group(form, b)])
        near_levels(form, b, twin)

    def send_facing(form):
        remote(x.at[form], across.at[form], sg.at[form], ry.at[form], facing, c).start()

    def spread(form, held, row):
        for k in range(groups) if form == 0 else spans:
            to = 4 * lax.rem(block + k, groups) + 2 * lax.rem(chip, 2)
            for e in range(2):
                dst = kv.at[0, row, e] if form == 0 else q.at[1, row]
                recv = rg.at[form, block]
                if k == 0:
                    either(core == e, held.at[form, e], dst, sg.at[form], recv, to + e, c)
                else:
                    remote(held.at[form, e], dst, sg.at[form], recv, to + e, c).start()

    def spread_facing(form):
        landed(x.at[form], ry.at[form])
        spread(form, across, facing)

    def forward_copy(form, g):
        held = kv.at[form, pl.ds(batch * g, batch), core]
        return remote(held, held, sf.at[form], rf.at[form, g], mate, c)

    def near_landed(form, g):
        if form == 0:
            landed(q.at[0, pl.ds(0, nc - 1), pl.ds(0, batch * piece)], rn.at[form, g])
        elif deep > 1:
            landed(q.at[0, pl.ds(0, (nc - 2) * batch // nc)], rn.at[form, g])

    def gather_landed(form, g):
        landed(q.at[0, pl.ds(0, batch)], rg.at[form, g])

    def forward(form, b):
        (gather_landed if form == 0 else near_landed)(form, group(form, b))
        forward_copy(form, group(form, b)).start()

    lax.fori_loop(1, nc, scatter, 0)
    send_facing(0)
    spread(0, x, r)
    bias_swap.start()

    for fetch in fetches[2:]:
        fetch.wait()
    for form, w in enumerate((ws, we)):
        wgt[form] = w[:, 3 * channels : 4 * channels].astype(F32).T.astype(BF16)

    key_bias = jnp.concatenate([penalty(2 * c), penalty(2 * c + 1)], axis=1)
    for h in range(heads):
        bias[0, h] = (bs[h].astype(F32) + key_bias) * LOG2E

    landed(scat.at[pl.ds(0, nc - 1)], rs)
    cross(0)
    spread_facing(0)
    cross(1)
    send_facing(1)

    bias_swap.wait_recv()
    for source, cols_at, t in ((be, mine, r), (be_in, other, mate)):
        row = penalty(t)
        for h in range(heads):
            bias[1, h, :, cols_at] = (source[h].astype(F32).T + row) * LOG2E


    def near_direct(b, carry):
        g = group(0, b)
        landed(q.at[0, pl.ds(0, batch), part(0)], ra.at[0, g])
        own = near_piece(0, g, c)
        for d in range(1, nc):
            remote(own, own, sc.at[0], rn.at[0, g], r, lax.rem(c + d, nc)).start()
        return carry

    lax.fori_loop(0, groups, near_direct, 0)

    def forward_rows(b, carry):
        forward(0, b)
        return carry

    lax.fori_loop(0, groups, forward_rows, 0)
    spread(1, x, r)
    for b in range(groups):
        near_twin(1, b)
    for b in range(groups):
        near_levels(1, b, c)

    scale = depth ** (-0.5) * LOG2E
    lane = lax.broadcasted_iota(jnp.int32, (tile, channels), 1)
    head_of = lane // depth
    ones = jnp.ones((2 * tile, channels), BF16)

    def project(form, w, g):
        rows = kv[form, pl.ds(batch * g, batch)].reshape(2 * batch * tile, channels)
        return nn(rows, w[:, channels : 3 * channels]).astype(BF16)

    def attend(form, w, g):
        held = pl.ds(batch * g, batch)
        both = projected[g] if form == 0 else project(form, w, g)
        rows = q[form, held].reshape(batch * tile, channels)
        queries = nn(rows, w[:, :channels]) * scale
        for i in range(batch):
            a = batch * g + i
            keys = both[2 * i * tile : 2 * (i + 1) * tile, :channels]
            values = both[2 * i * tile : 2 * (i + 1) * tile, channels:]
            query = queries[i * tile : (i + 1) * tile]
            chosen = [jnp.where(head_of == h, query, 0.0).astype(BF16) for h in range(heads)]
            scores = nt(jnp.concatenate(chosen, axis=0), keys)
            stats = jnp.zeros((tile, channels), F32)
            probs = []
            for h in range(heads):
                part = scores[h * tile : (h + 1) * tile] + bias[form, h]
                peak = jnp.max(part, axis=1, keepdims=True)
                probs.append(jnp.exp2(part - peak).astype(BF16))
                stats = jnp.where(lane == h, peak, stats)
            totals = nn(jnp.concatenate(probs, axis=0), jnp.concatenate([values, ones], axis=1))
            numer = jnp.zeros((tile, channels), F32)
            for h in range(heads):
                part = totals[h * tile : (h + 1) * tile]
                numer = jnp.where(head_of == h, part[:, :channels], numer)
                stats = jnp.where(lane == heads + h, part[:, channels:], stats)
            pn[form, a] = numer.T.astype(BF16)
            pst[form, a] = stats.T[: 2 * heads]

    def send_partial(form, a):
        if form == 0:
            to, b = lax.rem(a // per, deep), lax.rem(a, per)
            pairs = (rsn.at[lane_z, b], rsn_sem), (rss.at[lane_z, b], rss_sem)
            here, row, col = to == lane_z, r, lap * deep + to
        else:
            pairs = (ren.at[core, chip], ren_sem.at[core]), (res.at[core, chip], res_sem.at[core])
            here, row, col = a == r, a, c
        either(here, pn.at[form, a], pairs[0][0], spn.at[form], pairs[0][1], row, col)
        either(here, pst.at[form, a], pairs[1][0], sps.at[form], pairs[1][1], row, col)

    def send_twin_partial(g):
        @pl.when(g // side != lap)
        def _():
            rows, slot = pl.ds(batch * g, batch), lax.rem(g, side)
            remote(pn.at[0, rows], twn.at[slot], spn.at[0], twn_sem.at[slot], r, twin).start()
            remote(pst.at[0, rows], tws.at[slot], sps.at[0], tws_sem.at[slot], r, twin).start()

    def merge_twin(slot):
        landed(twn.at[slot], twn_sem.at[slot])
        landed(tws.at[slot], tws_sem.at[slot])
        for k in range(batch):
            a = batch * (lap * side + slot) + k
            numer, largest, denom = combine([pn[0, a], twn[slot, k]], [pst[0, a], tws[slot, k]])
            pn[0, a] = jnp.concatenate(numer, axis=0).astype(BF16)
            pst[0, a, :heads] = largest
            pst[0, a, heads:] = denom
            send_partial(0, a)

    def combine(parts, stats):
        peaks = [s[:heads] for s in stats]
        largest = functools.reduce(jnp.maximum, peaks)
        factors = [jnp.exp2(p - largest) for p in peaks]
        denom = sum(f * s[heads:] for f, s in zip(factors, stats))
        rows = []
        for h in range(heads):
            pick = slice(h * depth, (h + 1) * depth)
            rows.append(sum(f[h : h + 1] * p[pick].astype(F32) for f, p in zip(factors, parts)))
        return rows, largest, denom

    def divided(parts, stats):
        rows, _, denom = combine(parts, stats)
        return jnp.concatenate([row / denom[h : h + 1] for h, row in enumerate(rows)], axis=0)

    def run_form(form, w):
        if form == 0:
            def ahead(b, carry):
                g = group(0, b)
                forward_copy(0, g).wait_recv()
                projected[g] = project(0, w, g)
                return carry

            lax.fori_loop(0, groups, ahead, 0)
        else:
            forward(form, 0)

        def step(b, carry):
            g = group(form, b)
            if form == 0:
                @pl.when(b == 0)
                def _():
                    spread_facing(1)
                relay(1, b)
            if form == 0:
                near_landed(form, g)
            else:
                @pl.when(b + 1 < groups)
                def _():
                    forward(form, b + 1)
                gather_landed(form, g)
                forward_copy(form, g).wait_recv()
            attend(form, w, g)
            if form == 0:
                send_twin_partial(g)
            else:
                @pl.when((b >= MERGE) & (b < MERGE + groups // 2))
                def _():
                    merge_twin(b - MERGE)
                for k in range(batch):
                    send_partial(1, batch * g + k)
            return carry

        lax.fori_loop(0, groups, step, 0)

    def finish(form, attended, rows, weight, mask):
        gate = nt(wgt[form], rows)
        gated = jax.nn.sigmoid(gate) * attended * mask
        return nn(gated.T.astype(BF16), weight).astype(BF16)

    run_form(0, ws)
    run_form(1, we)

    def mask_scalar(k, a):
        at = offs[k] + a
        return tms[at // tile, lax.rem(at, tile)].astype(F32)

    landed(rsn, rsn_sem)
    landed(rss, rss_sem)
    for b in range(per):
        a = per * c + b
        attended = divided([rsn[g, b] for g in range(deep)], [rss[g, b] for g in range(deep)])
        mask = mask_row(r) * mask_scalar(0, a)
        out_s[b] = finish(0, attended, q[0, a], wso[...], mask)

    for e in range(2):
        landed(ren.at[e], ren_sem.at[e])
        landed(res.at[e], res_sem.at[e])
        attended = divided([ren[e, m] for m in range(nc)], [res[e, m] for m in range(nc)])
        mask = mask_row(2 * c + e) * mask_scalar(1, r)
        out_e[0, e * tile : (e + 1) * tile, :] = finish(1, attended, x[1, e], weo[...], mask)

    bias_swap.wait_send()
    gone(scat.at[pl.ds(0, nc - 1)], ss)
    for form in range(2):
        gone(q.at[0, pl.ds(0, n - 1), part(0)], sa.at[form])
        gone(q.at[0], sg.at[form])
        gone(q.at[0, pl.ds(0, (nc - 1) * per)], sc.at[form])
        gone(q.at[0], sf.at[form])
        remote_count = n - per if form == 0 else n - 1
        gone(pn.at[form, pl.ds(0, remote_count)], spn.at[form])
        gone(pst.at[form, pl.ds(0, remote_count)], sps.at[form])


def local(z_rows, z_cols, bias_start, bias_end, w_start_in, w_start_out, w_end_in, w_end_out, token_mask, offsets):
    n, nc = lax.axis_size("row"), lax.axis_size("col")
    heads, tile, span = bias_start.shape
    channels = z_rows.shape[2]
    per = n // nc
    groups = n // min(BATCH, n)
    vmem = pl.BlockSpec(memory_space=pltpu.VMEM)
    smem = pl.BlockSpec(memory_space=pltpu.SMEM)
    dma = pltpu.SemaphoreType.DMA
    return pl.pallas_call(
        functools.partial(kernel, n, nc, heads),
        out_shape=(
            jax.ShapeDtypeStruct((per, tile, channels), BF16),
            jax.ShapeDtypeStruct((1, span, channels), BF16),
        ),
        in_specs=[pl.BlockSpec(memory_space=pl.ANY)] * 9 + [smem],
        out_specs=(vmem, vmem),
        scratch_shapes=[
            pltpu.VMEM(z_rows.shape, BF16),
            pltpu.VMEM(z_cols.shape, BF16),
            pltpu.VMEM(bias_start.shape, BF16),
            pltpu.VMEM((heads, tile, tile), BF16),
            pltpu.VMEM(w_start_in.shape, BF16),
            pltpu.VMEM(w_start_out.shape, BF16),
            pltpu.VMEM(w_end_in.shape, BF16),
            pltpu.VMEM(w_end_out.shape, BF16),
            pltpu.VMEM((n, tile), jnp.int32),
            pltpu.SMEM((n, tile), jnp.int32),
            dma((10,)),
            pltpu.VMEM((2, 2, tile, channels), BF16),
            pltpu.VMEM((2, 2, tile, channels), BF16),
            pltpu.VMEM((nc, 2, 2, tile // nc, channels), BF16),
            pltpu.VMEM((2, n, 2, tile, channels), BF16),
            pltpu.VMEM((2, n, tile, channels), BF16),
            pltpu.VMEM((2, heads, tile, span), F32),
            pltpu.VMEM((2, channels, channels), BF16),
            pltpu.VMEM((heads, tile, tile), BF16),
            pltpu.VMEM((2, n, channels, tile), BF16),
            pltpu.VMEM((2, n, 2 * heads, tile), F32),
            pltpu.VMEM((nc // 2, per, channels, tile), BF16),
            pltpu.VMEM((nc // 2, per, 2 * heads, tile), F32),
            pltpu.VMEM((2, nc, channels, tile), BF16),
            pltpu.VMEM((2, nc, 2 * heads, tile), F32),
            pltpu.VMEM((groups // 2, n // groups, channels, tile), BF16),
            pltpu.VMEM((groups // 2, n // groups, 2 * heads, tile), F32),
            pltpu.VMEM((groups, n // groups * span, 2 * channels), BF16),
            dma, dma((2,)), dma((2,)), dma((2,)), dma((2,)), dma((2,)), dma((2,)), dma,
            dma, dma((2, groups)), dma((2, groups)), dma((2,)), dma((2, groups)), dma((2, groups)), dma((2, groups)),
            dma, dma, dma((2,)), dma((2,)), dma((groups // 2,)), dma((groups // 2,)), dma,
        ],
        compiler_params=pltpu.CompilerParams(
            collective_id=0, has_side_effects=True, vmem_limit_bytes=62 * 1024 * 1024
        ),
        name="triangle_attention",
    )(
        z_rows, z_cols, bias_start, bias_end, w_start_in, w_start_out, w_end_in, w_end_out,
        token_mask.reshape(-1, tile), offsets,
    )


def solution(mesh):
    return jax.shard_map(
        local,
        mesh=mesh,
        in_specs=(
            P("row", "col", None),
            P("row", "col", None),
            P(None, "row", "col"),
            P(None, "row", "col"),
            P(),
            P(),
            P(),
            P(),
            P(),
            P(),
        ),
        out_specs=(P("col", "row", None), P("row", "col", None)),
        check_vma=False,
    )
```

```python
import functools
import math

import jax
import jax.numpy as jnp
from jax import lax
from jax.experimental import pallas as pl
from jax.experimental.pallas import tpu as pltpu
from jax.sharding import PartitionSpec as P

MESH = pl.DeviceIdType.MESH
LOG2E = math.log2(math.e)
BATCH = 4
MERGE = 2
F32 = jnp.float32
BF16 = jnp.bfloat16


def nn(a, b):
    return lax.dot_general(a, b, (((1,), (0,)), ((), ())), preferred_element_type=F32)


def nt(a, b):
    return lax.dot_general(a, b, (((1,), (1,)), ((), ())), preferred_element_type=F32)


def normalize(block):
    values = block.astype(F32)
    center = values - jnp.mean(values, axis=-1, keepdims=True)
    spread = jnp.mean(center * center, axis=-1, keepdims=True)
    return (center * lax.rsqrt(spread + 1e-05)).astype(BF16)


def kernel(
    n, nc, heads,
    zr_in, zc_in, bs_in, be_far, ws_in, wso_in, we_in, weo_in, tm_in, offs,
    out_s, out_e,
    zr, zc, bs, be, ws, wso, we, weo, tm, tms, got,
    x, across, scat, kv, q, bias, wgt, be_in, pn, pst, rsn, rss, ren, res, twn, tws, projected,
    ss, sa, sg, sc, sf, spn, sps, sb,
    rs, ra, rg, ry, rt, rn, rf, rsn_sem, rss_sem, ren_sem, res_sem, twn_sem, tws_sem, rb,
):
    r = lax.axis_index("row")
    c = lax.axis_index("col")
    core = lax.rem(r, 2)
    chip = r // 2
    mate = r + 1 - 2 * core
    tile = tm.shape[1]
    channels = zr.shape[2]
    batch = min(BATCH, n)
    depth = channels // heads
    per = n // nc
    mine = pl.ds(pl.multiple_of(core * tile, tile), tile)
    other = pl.ds(pl.multiple_of((1 - core) * tile, tile), tile)
    deep = nc // 2
    lap, lane_z = c // deep, lax.rem(c, deep)
    twin = (1 - lap) * deep + lane_z

    def level(d):
        return lap * deep + lax.rem(lane_z + d, deep)

    groups = n // batch
    piece = tile // nc
    block = chip // 2
    facing = r + 2 - 4 * lax.rem(chip, 2)

    side = groups // 2
    spans = [3, 1, 2, 0] if groups == 4 else [k % groups for k in range(1, groups + 1)]

    def group(form, b):
        if form == 0:
            return lax.rem(block + groups - b, groups)
        span = spans[0]
        for k in range(1, groups):
            span = jnp.where(b == k, spans[k], span)
        return lax.rem(block + groups - span, groups)

    def along(u):
        return 2 * lax.rem(block + u // 2, groups) + lax.rem(chip + u, 2)

    def mask_row(t):
        return tm[pl.ds(t, 1), :].astype(F32)

    def penalty(t):
        return (mask_row(t) - 1.0) * 1e9

    def part(p):
        return pl.ds(pl.multiple_of(p * piece, piece), piece)

    fetches = [
        pltpu.make_async_copy(src, dst, got.at[k])
        for k, (src, dst) in enumerate((
            (zr_in, zr), (zc_in, zc), (ws_in, ws), (we_in, we), (tm_in, tm), (bs_in, bs),
            (be_far.at[:, :, mine], be), (wso_in, wso), (weo_in, weo), (tm_in, tms),
        ))
    ]
    for fetch in fetches[:2]:
        fetch.start()

    barrier = pltpu.get_barrier_semaphore()

    def greet(row, col):
        pl.semaphore_signal(barrier, inc=1, device_id=(row, col), device_id_type=MESH)

    def greet_row(d, carry):
        greet(lax.rem(r + d, n), c)
        return carry

    def greet_col(d, carry):
        greet(r, lax.rem(c + d, nc))
        return carry

    for d in sorted(range(1, n), key=lambda d: -min(d, n - d)):
        greet_row(d, 0)
    for d in sorted(range(1, nc), key=lambda d: -min(d, nc - d)):
        greet_col(d, 0)

    for fetch in fetches[2:]:
        fetch.start()

    fetches[0].wait()
    x[0] = normalize(zr[0]).reshape(2, tile, channels)
    fetches[1].wait()
    x[1] = normalize(zc[0]).reshape(2, tile, channels)
    for form in range(2):
        for e in range(2):
            scat[c, form, e] = x[form, e, part(c), :]

    pl.semaphore_wait(barrier, n - 1 + nc - 1)

    def remote(src, dst, send, recv, row, col):
        return pltpu.make_async_remote_copy(
            src_ref=src, dst_ref=dst, send_sem=send, recv_sem=recv,
            device_id=(row, col), device_id_type=MESH,
        )

    def either(here, src, dst, send, recv, row, col):
        @pl.when(here)
        def _():
            pltpu.make_async_copy(src, dst, recv).start()
        @pl.when(jnp.logical_not(here))
        def _():
            remote(src, dst, send, recv, row, col).start()

    bias_swap = remote(
        be_far.at[:, :, other], be_in, sb, rb, mate, c
    )

    def landed(dst, recv):
        remote(dst, dst, sb, recv, mate, c).wait_recv()

    def gone(src, send):
        remote(src, src, send, rb, mate, c).wait_send()

    def scatter(d, carry):
        to = lax.rem(c + d, nc)
        remote(x.at[:, :, part(to)], scat.at[c], ss, rs, r, to).start()
        return carry

    def cross(form):
        def step(u, carry):
            to = along(u)
            for e in range(2):
                dst = q.at[0, r, part(c)] if form == 0 else kv.at[1, r, e, part(c)]
                src = scat.at[to, form, e]
                either((u == 0) & (core == e), src, dst, sa.at[form], ra.at[form, block], 2 * to + e, c)
            return carry
        lax.fori_loop(0, nc, step, 0)

    def near_piece(form, g, p):
        rows = pl.ds(batch * g, batch)
        return q.at[0, rows, part(p)] if form == 0 else kv.at[1, rows, core, part(p)]

    def near_twin(form, b):
        g = group(form, b)
        landed(q.at[0, pl.ds(0, batch), part(0)], ra.at[form, g])
        own = near_piece(form, g, c)
        remote(own, own, sc.at[form], rt.at[form, g], r, twin).start()

    def near_levels(form, b, held):
        g = group(form, b)
        piece_ref = near_piece(form, g, held)
        for d in range(1, deep):
            remote(piece_ref, piece_ref, sc.at[form], rn.at[form, g], r, level(d)).start()

    def relay(form, b):
        landed(near_piece(form, group(form, b), twin), rt.at[form, group(form, b)])
        near_levels(form, b, twin)

    def send_facing(form):
        remote(x.at[form], across.at[form], sg.at[form], ry.at[form], facing, c).start()

    def spread(form, held, row):
        for k in range(groups) if form == 0 else spans:
            to = 4 * lax.rem(block + k, groups) + 2 * lax.rem(chip, 2)
            for e in range(2):
                dst = kv.at[0, row, e] if form == 0 else q.at[1, row]
                recv = rg.at[form, block]
                if k == 0:
                    either(core == e, held.at[form, e], dst, sg.at[form], recv, to + e, c)
                else:
                    remote(held.at[form, e], dst, sg.at[form], recv, to + e, c).start()

    def spread_facing(form):
        landed(x.at[form], ry.at[form])
        spread(form, across, facing)

    def forward_copy(form, g):
        held = kv.at[form, pl.ds(batch * g, batch), core]
        return remote(held, held, sf.at[form], rf.at[form, g], mate, c)

    def near_landed(form, g):
        if form == 0:
            landed(q.at[0, pl.ds(0, batch // 2)], rn.at[form, g])
        elif deep > 1:
            landed(q.at[0, pl.ds(0, (nc - 2) * batch // nc)], rn.at[form, g])

    def gather_landed(form, g):
        landed(q.at[0, pl.ds(0, batch)], rg.at[form, g])

    def forward(form, b):
        (gather_landed if form == 0 else near_landed)(form, group(form, b))
        forward_copy(form, group(form, b)).start()

    lax.fori_loop(1, nc, scatter, 0)
    send_facing(0)
    spread(0, x, r)
    bias_swap.start()

    for fetch in fetches[2:]:
        fetch.wait()
    for form, w in enumerate((ws, we)):
        wgt[form] = w[:, 3 * channels : 4 * channels].astype(F32).T.astype(BF16)

    key_bias = jnp.concatenate([penalty(2 * c), penalty(2 * c + 1)], axis=1)
    for h in range(heads):
        bias[0, h] = (bs[h].astype(F32) + key_bias) * LOG2E

    landed(scat.at[pl.ds(0, nc - 1)], rs)
    cross(0)
    cross(1)
    spread_facing(0)
    send_facing(1)

    def near_level(b, carry):
        g = group(0, b)
        landed(q.at[0, pl.ds(0, batch), part(0)], ra.at[0, g])
        own = near_piece(0, g, c)
        for d in range(1, deep):
            remote(own, own, sc.at[0], rt.at[0, g], r, level(d)).start()
        remote(own, own, sc.at[0], rn.at[0, g], r, twin).start()
        return carry

    def level_to_twin(b):
        g = group(0, b)
        landed(q.at[0, pl.ds(0, (deep - 1) * batch), part(0)], rt.at[0, g])
        for d in range(1, deep):
            held = near_piece(0, g, level(d))
            remote(held, held, sc.at[0], rn.at[0, g], r, twin).start()

    def forward_rows(b, carry):
        forward(0, b)
        return carry

    lax.fori_loop(0, groups, near_level, 0)
    lax.fori_loop(0, groups, forward_rows, 0)
    for b in range(groups):
        near_twin(1, b)
    for b in range(groups):
        near_levels(1, b, c)
    level_to_twin(0)
    level_to_twin(1)
    level_to_twin(2)
    level_to_twin(3)
    spread(1, x, r)

    scale = depth ** (-0.5) * LOG2E
    lane = lax.broadcasted_iota(jnp.int32, (tile, channels), 1)
    head_of = lane // depth
    ones = jnp.ones((2 * tile, channels), BF16)

    def project(form, w, g):
        rows = kv[form, pl.ds(batch * g, batch)].reshape(2 * batch * tile, channels)
        return nn(rows, w[:, channels : 3 * channels]).astype(BF16)

    def attend(form, w, g):
        held = pl.ds(batch * g, batch)
        both = projected[g] if form == 0 else project(form, w, g)
        rows = q[form, held].reshape(batch * tile, channels)
        queries = nn(rows, w[:, :channels]) * scale
        for i in range(batch):
            a = batch * g + i
            keys = both[2 * i * tile : 2 * (i + 1) * tile, :channels]
            values = both[2 * i * tile : 2 * (i + 1) * tile, channels:]
            query = queries[i * tile : (i + 1) * tile]
            chosen = [jnp.where(head_of == h, query, 0.0).astype(BF16) for h in range(heads)]
            scores = nt(jnp.concatenate(chosen, axis=0), keys)
            stats = jnp.zeros((tile, channels), F32)
            probs = []
            for h in range(heads):
                part = scores[h * tile : (h + 1) * tile] + bias[form, h]
                peak = jnp.max(part, axis=1, keepdims=True)
                probs.append(jnp.exp2(part - peak).astype(BF16))
                stats = jnp.where(lane == h, peak, stats)
            totals = nn(jnp.concatenate(probs, axis=0), jnp.concatenate([values, ones], axis=1))
            numer = jnp.zeros((tile, channels), F32)
            for h in range(heads):
                part = totals[h * tile : (h + 1) * tile]
                numer = jnp.where(head_of == h, part[:, :channels], numer)
                stats = jnp.where(lane == heads + h, part[:, channels:], stats)
            pn[form, a] = numer.T.astype(BF16)
            pst[form, a] = stats.T[: 2 * heads]

    def send_partial(form, a):
        if form == 0:
            to, b = lax.rem(a // per, deep), lax.rem(a, per)
            pairs = (rsn.at[lane_z, b], rsn_sem), (rss.at[lane_z, b], rss_sem)
            here, row, col = to == lane_z, r, lap * deep + to
        else:
            pairs = (ren.at[core, chip], ren_sem.at[core]), (res.at[core, chip], res_sem.at[core])
            here, row, col = a == r, a, c
        either(here, pn.at[form, a], pairs[0][0], spn.at[form], pairs[0][1], row, col)
        either(here, pst.at[form, a], pairs[1][0], sps.at[form], pairs[1][1], row, col)

    def send_twin_partial(g):
        @pl.when(g // side != lap)
        def _():
            rows, slot = pl.ds(batch * g, batch), lax.rem(g, side)
            remote(pn.at[0, rows], twn.at[slot], spn.at[0], twn_sem.at[slot], r, twin).start()
            remote(pst.at[0, rows], tws.at[slot], sps.at[0], tws_sem.at[slot], r, twin).start()

    def merge_twin(slot):
        landed(twn.at[slot], twn_sem.at[slot])
        landed(tws.at[slot], tws_sem.at[slot])
        for k in range(batch):
            a = batch * (lap * side + slot) + k
            numer, largest, denom = combine([pn[0, a], twn[slot, k]], [pst[0, a], tws[slot, k]])
            pn[0, a] = jnp.concatenate(numer, axis=0).astype(BF16)
            pst[0, a, :heads] = largest
            pst[0, a, heads:] = denom
            send_partial(0, a)

    def combine(parts, stats):
        peaks = [s[:heads] for s in stats]
        largest = functools.reduce(jnp.maximum, peaks)
        factors = [jnp.exp2(p - largest) for p in peaks]
        denom = sum(f * s[heads:] for f, s in zip(factors, stats))
        rows = []
        for h in range(heads):
            pick = slice(h * depth, (h + 1) * depth)
            rows.append(sum(f[h : h + 1] * p[pick].astype(F32) for f, p in zip(factors, parts)))
        return rows, largest, denom

    def divided(parts, stats):
        rows, _, denom = combine(parts, stats)
        return jnp.concatenate([row / denom[h : h + 1] for h, row in enumerate(rows)], axis=0)

    def run_form(form, w):
        if form == 0:
            def ahead(b, carry):
                g = group(0, b)
                forward_copy(0, g).wait_recv()
                projected[g] = project(0, w, g)
                return carry

            lax.fori_loop(0, groups, ahead, 0)
        else:
            forward(form, 0)

        def step(b, carry):
            g = group(form, b)
            if form == 0:
                @pl.when(b == 0)
                def _():
                    spread_facing(1)
                relay(1, b)
            if form == 0:
                near_landed(form, g)
            else:
                @pl.when(b + 1 < groups)
                def _():
                    forward(form, b + 1)
                gather_landed(form, g)
                forward_copy(form, g).wait_recv()
            attend(form, w, g)
            if form == 0:
                send_twin_partial(g)
            else:
                for k in range(batch):
                    send_partial(1, batch * g + k)
                @pl.when((b >= MERGE) & (b < MERGE + groups // 2))
                def _():
                    merge_twin(b - MERGE)
            return carry

        lax.fori_loop(0, groups, step, 0)

    def finish(form, attended, rows, weight, mask):
        gate = nt(wgt[form], rows)
        gated = jax.nn.sigmoid(gate) * attended * mask
        return nn(gated.T.astype(BF16), weight).astype(BF16)

    run_form(0, ws)
    bias_swap.wait_recv()
    for source, cols_at, t in ((be, mine, r), (be_in, other, mate)):
        row = penalty(t)
        for h in range(heads):
            bias[1, h, :, cols_at] = (source[h].astype(F32).T + row) * LOG2E


    run_form(1, we)

    def mask_scalar(k, a):
        at = offs[k] + a
        return tms[at // tile, lax.rem(at, tile)].astype(F32)

    landed(rsn, rsn_sem)
    landed(rss, rss_sem)
    for b in range(per):
        a = per * c + b
        attended = divided([rsn[g, b] for g in range(deep)], [rss[g, b] for g in range(deep)])
        mask = mask_row(r) * mask_scalar(0, a)
        out_s[b] = finish(0, attended, q[0, a], wso[...], mask)

    for e in range(2):
        landed(ren.at[e], ren_sem.at[e])
        landed(res.at[e], res_sem.at[e])
        attended = divided([ren[e, m] for m in range(nc)], [res[e, m] for m in range(nc)])
        mask = mask_row(2 * c + e) * mask_scalar(1, r)
        out_e[0, e * tile : (e + 1) * tile, :] = finish(1, attended, x[1, e], weo[...], mask)

    bias_swap.wait_send()
    gone(scat.at[pl.ds(0, nc - 1)], ss)
    for form in range(2):
        gone(q.at[0, pl.ds(0, n - 1), part(0)], sa.at[form])
        gone(q.at[0], sg.at[form])
        gone(q.at[0, pl.ds(0, (nc - 1) * per)], sc.at[form])
        gone(q.at[0], sf.at[form])
        remote_count = n - per if form == 0 else n - 1
        gone(pn.at[form, pl.ds(0, remote_count)], spn.at[form])
        gone(pst.at[form, pl.ds(0, remote_count)], sps.at[form])


def local(z_rows, z_cols, bias_start, bias_end, w_start_in, w_start_out, w_end_in, w_end_out, token_mask, offsets):
    n, nc = lax.axis_size("row"), lax.axis_size("col")
    heads, tile, span = bias_start.shape
    channels = z_rows.shape[2]
    per = n // nc
    groups = n // min(BATCH, n)
    vmem = pl.BlockSpec(memory_space=pltpu.VMEM)
    smem = pl.BlockSpec(memory_space=pltpu.SMEM)
    dma = pltpu.SemaphoreType.DMA
    return pl.pallas_call(
        functools.partial(kernel, n, nc, heads),
        out_shape=(
            jax.ShapeDtypeStruct((per, tile, channels), BF16),
            jax.ShapeDtypeStruct((1, span, channels), BF16),
        ),
        in_specs=[pl.BlockSpec(memory_space=pl.ANY)] * 9 + [smem],
        out_specs=(vmem, vmem),
        scratch_shapes=[
            pltpu.VMEM(z_rows.shape, BF16),
            pltpu.VMEM(z_cols.shape, BF16),
            pltpu.VMEM(bias_start.shape, BF16),
            pltpu.VMEM((heads, tile, tile), BF16),
            pltpu.VMEM(w_start_in.shape, BF16),
            pltpu.VMEM(w_start_out.shape, BF16),
            pltpu.VMEM(w_end_in.shape, BF16),
            pltpu.VMEM(w_end_out.shape, BF16),
            pltpu.VMEM((n, tile), jnp.int32),
            pltpu.SMEM((n, tile), jnp.int32),
            dma((10,)),
            pltpu.VMEM((2, 2, tile, channels), BF16),
            pltpu.VMEM((2, 2, tile, channels), BF16),
            pltpu.VMEM((nc, 2, 2, tile // nc, channels), BF16),
            pltpu.VMEM((2, n, 2, tile, channels), BF16),
            pltpu.VMEM((2, n, tile, channels), BF16),
            pltpu.VMEM((2, heads, tile, span), F32),
            pltpu.VMEM((2, channels, channels), BF16),
            pltpu.VMEM((heads, tile, tile), BF16),
            pltpu.VMEM((2, n, channels, tile), BF16),
            pltpu.VMEM((2, n, 2 * heads, tile), F32),
            pltpu.VMEM((nc // 2, per, channels, tile), BF16),
            pltpu.VMEM((nc // 2, per, 2 * heads, tile), F32),
            pltpu.VMEM((2, nc, channels, tile), BF16),
            pltpu.VMEM((2, nc, 2 * heads, tile), F32),
            pltpu.VMEM((groups // 2, n // groups, channels, tile), BF16),
            pltpu.VMEM((groups // 2, n // groups, 2 * heads, tile), F32),
            pltpu.VMEM((groups, n // groups * span, 2 * channels), BF16),
            dma, dma((2,)), dma((2,)), dma((2,)), dma((2,)), dma((2,)), dma((2,)), dma,
            dma, dma((2, groups)), dma((2, groups)), dma((2,)), dma((2, groups)), dma((2, groups)), dma((2, groups)),
            dma, dma, dma((2,)), dma((2,)), dma((groups // 2,)), dma((groups // 2,)), dma,
        ],
        compiler_params=pltpu.CompilerParams(
            collective_id=0, has_side_effects=True, vmem_limit_bytes=62 * 1024 * 1024
        ),
        name="triangle_attention",
    )(
        z_rows, z_cols, bias_start, bias_end, w_start_in, w_start_out, w_end_in, w_end_out,
        token_mask.reshape(-1, tile), offsets,
    )


def solution(mesh):
    return jax.shard_map(
        local,
        mesh=mesh,
        in_specs=(
            P("row", "col", None),
            P("row", "col", None),
            P(None, "row", "col"),
            P(None, "row", "col"),
            P(),
            P(),
            P(),
            P(),
            P(),
            P(),
        ),
        out_specs=(P("col", "row", None), P("row", "col", None)),
        check_vma=False,
    )
```

```python
import functools
import math

import jax
import jax.numpy as jnp
from jax import lax
from jax.experimental import pallas as pl
from jax.experimental.pallas import tpu as pltpu
from jax.sharding import PartitionSpec as P

MESH = pl.DeviceIdType.MESH
LOG2E = math.log2(math.e)
BATCH = 4
MERGE = 2
F32 = jnp.float32
BF16 = jnp.bfloat16


def nn(a, b):
    return lax.dot_general(a, b, (((1,), (0,)), ((), ())), preferred_element_type=F32)


def nt(a, b):
    return lax.dot_general(a, b, (((1,), (1,)), ((), ())), preferred_element_type=F32)


def normalize(block):
    values = block.astype(F32)
    center = values - jnp.mean(values, axis=-1, keepdims=True)
    spread = jnp.mean(center * center, axis=-1, keepdims=True)
    return (center * lax.rsqrt(spread + 1e-05)).astype(BF16)


def kernel(
    n, nc, heads,
    zr_in, zc_in, bs_in, be_far, ws_in, wso_in, we_in, weo_in, tm_in, offs,
    out_s, out_e,
    zr, zc, bs, be, ws, wso, we, weo, tm, tms, got,
    x, across, scat, kv, q, bias, wgt, be_in, pn, pst, rsn, rss, ren, res, twn, tws, projected,
    ss, sa, sg, sc, sf, spn, sps, sb,
    rs, ra, rg, ry, rt, rn, rf, rsn_sem, rss_sem, ren_sem, res_sem, twn_sem, tws_sem, rb,
):
    r = lax.axis_index("row")
    c = lax.axis_index("col")
    core = lax.rem(r, 2)
    chip = r // 2
    mate = r + 1 - 2 * core
    tile = tm.shape[1]
    channels = zr.shape[2]
    batch = min(BATCH, n)
    depth = channels // heads
    per = n // nc
    mine = pl.ds(pl.multiple_of(core * tile, tile), tile)
    other = pl.ds(pl.multiple_of((1 - core) * tile, tile), tile)
    deep = nc // 2
    lap, lane_z = c // deep, lax.rem(c, deep)
    twin = (1 - lap) * deep + lane_z

    def level(d):
        return lap * deep + lax.rem(lane_z + d, deep)

    groups = n // batch
    piece = tile // nc
    block = chip // 2
    facing = r + 2 - 4 * lax.rem(chip, 2)

    side = groups // 2
    spans = [3, 1, 2, 0] if groups == 4 else [k % groups for k in range(1, groups + 1)]

    def group(form, b):
        if form == 0:
            return lax.rem(block + groups - b, groups)
        span = spans[0]
        for k in range(1, groups):
            span = jnp.where(b == k, spans[k], span)
        return lax.rem(block + groups - span, groups)

    def along(u):
        return 2 * lax.rem(block + u // 2, groups) + lax.rem(chip + u, 2)

    def mask_row(t):
        return tm[pl.ds(t, 1), :].astype(F32)

    def penalty(t):
        return (mask_row(t) - 1.0) * 1e9

    def part(p):
        return pl.ds(pl.multiple_of(p * piece, piece), piece)

    fetches = [
        pltpu.make_async_copy(src, dst, got.at[k])
        for k, (src, dst) in enumerate((
            (zr_in, zr), (zc_in, zc), (ws_in, ws), (we_in, we), (tm_in, tm), (bs_in, bs),
            (be_far.at[:, :, mine], be), (wso_in, wso), (weo_in, weo), (tm_in, tms),
        ))
    ]
    for fetch in fetches[:2]:
        fetch.start()

    barrier = pltpu.get_barrier_semaphore()

    def greet(row, col):
        pl.semaphore_signal(barrier, inc=1, device_id=(row, col), device_id_type=MESH)

    def greet_row(d, carry):
        greet(lax.rem(r + d, n), c)
        return carry

    def greet_col(d, carry):
        greet(r, lax.rem(c + d, nc))
        return carry

    for d in sorted(range(1, n), key=lambda d: -min(d, n - d)):
        greet_row(d, 0)
    for d in sorted(range(1, nc), key=lambda d: -min(d, nc - d)):
        greet_col(d, 0)

    for fetch in fetches[2:]:
        fetch.start()

    fetches[0].wait()
    x[0] = normalize(zr[0]).reshape(2, tile, channels)
    fetches[1].wait()
    x[1] = normalize(zc[0]).reshape(2, tile, channels)
    for form in range(2):
        for e in range(2):
            scat[c, form, e] = x[form, e, part(c), :]

    pl.semaphore_wait(barrier, n - 1 + nc - 1)

    def remote(src, dst, send, recv, row, col):
        return pltpu.make_async_remote_copy(
            src_ref=src, dst_ref=dst, send_sem=send, recv_sem=recv,
            device_id=(row, col), device_id_type=MESH,
        )

    def either(here, src, dst, send, recv, row, col):
        @pl.when(here)
        def _():
            pltpu.make_async_copy(src, dst, recv).start()
        @pl.when(jnp.logical_not(here))
        def _():
            remote(src, dst, send, recv, row, col).start()

    bias_swap = remote(
        be_far.at[:, :, other], be_in, sb, rb, mate, c
    )

    def landed(dst, recv):
        remote(dst, dst, sb, recv, mate, c).wait_recv()

    def gone(src, send):
        remote(src, src, send, rb, mate, c).wait_send()

    def scatter(d, carry):
        to = lax.rem(c + d, nc)
        remote(x.at[:, :, part(to)], scat.at[c], ss, rs, r, to).start()
        return carry

    def cross(form):
        def step(u, carry):
            to = along(u)
            for e in range(2):
                dst = q.at[0, r, part(c)] if form == 0 else kv.at[1, r, e, part(c)]
                src = scat.at[to, form, e]
                either((u == 0) & (core == e), src, dst, sa.at[form], ra.at[form, block], 2 * to + e, c)
            return carry
        lax.fori_loop(0, nc, step, 0)

    def near_piece(form, g, p):
        rows = pl.ds(batch * g, batch)
        return q.at[0, rows, part(p)] if form == 0 else kv.at[1, rows, core, part(p)]

    def near_twin(form, b):
        g = group(form, b)
        landed(q.at[0, pl.ds(0, batch), part(0)], ra.at[form, g])
        own = near_piece(form, g, c)
        remote(own, own, sc.at[form], rt.at[form, g], r, twin).start()

    def near_levels(form, b, held):
        g = group(form, b)
        piece_ref = near_piece(form, g, held)
        for d in range(1, deep):
            remote(piece_ref, piece_ref, sc.at[form], rn.at[form, g], r, level(d)).start()

    def relay(form, b):
        landed(near_piece(form, group(form, b), twin), rt.at[form, group(form, b)])
        near_levels(form, b, twin)

    def send_facing(form):
        remote(x.at[form], across.at[form], sg.at[form], ry.at[form], facing, c).start()

    def spread(form, held, row):
        for k in range(groups) if form == 0 else spans:
            to = 4 * lax.rem(block + k, groups) + 2 * lax.rem(chip, 2)
            for e in range(2):
                dst = kv.at[0, row, e] if form == 0 else q.at[1, row]
                recv = rg.at[form, block]
                if k == 0:
                    either(core == e, held.at[form, e], dst, sg.at[form], recv, to + e, c)
                else:
                    remote(held.at[form, e], dst, sg.at[form], recv, to + e, c).start()

    def spread_facing(form):
        landed(x.at[form], ry.at[form])
        spread(form, across, facing)

    def forward_copy(form, g):
        held = kv.at[form, pl.ds(batch * g, batch), core]
        return remote(held, held, sf.at[form], rf.at[form, g], mate, c)

    def near_landed(form, g):
        if form == 0:
            landed(q.at[0, pl.ds(0, batch // 2)], rn.at[form, g])
        elif deep > 1:
            landed(q.at[0, pl.ds(0, (nc - 2) * batch // nc)], rn.at[form, g])

    def gather_landed(form, g):
        landed(q.at[0, pl.ds(0, batch)], rg.at[form, g])

    def forward(form, b):
        (gather_landed if form == 0 else near_landed)(form, group(form, b))
        forward_copy(form, group(form, b)).start()

    lax.fori_loop(1, nc, scatter, 0)
    send_facing(0)
    spread(0, x, r)
    bias_swap.start()

    for fetch in fetches[2:]:
        fetch.wait()
    for form, w in enumerate((ws, we)):
        wgt[form] = w[:, 3 * channels : 4 * channels].astype(F32).T.astype(BF16)

    key_bias = jnp.concatenate([penalty(2 * c), penalty(2 * c + 1)], axis=1)
    for h in range(heads):
        bias[0, h] = (bs[h].astype(F32) + key_bias) * LOG2E

    landed(scat.at[pl.ds(0, nc - 1)], rs)
    cross(0)
    cross(1)
    spread_facing(0)
    send_facing(1)

    def near_level(b, carry):
        g = group(0, b)
        landed(q.at[0, pl.ds(0, batch), part(0)], ra.at[0, g])
        own = near_piece(0, g, c)
        for d in range(1, deep):
            remote(own, own, sc.at[0], rt.at[0, g], r, level(d)).start()
        remote(own, own, sc.at[0], rn.at[0, g], r, twin).start()
        return carry

    def level_to_twin(b):
        g = group(0, b)
        landed(q.at[0, pl.ds(0, (deep - 1) * batch), part(0)], rt.at[0, g])
        for d in range(1, deep):
            held = near_piece(0, g, level(d))
            remote(held, held, sc.at[0], rn.at[0, g], r, twin).start()

    def forward_rows(b, carry):
        forward(0, b)
        return carry

    lax.fori_loop(0, groups, near_level, 0)
    lax.fori_loop(0, groups, forward_rows, 0)
    for b in range(groups):
        near_twin(1, b)
    for b in range(groups):
        near_levels(1, b, c)

    scale = depth ** (-0.5) * LOG2E
    lane = lax.broadcasted_iota(jnp.int32, (tile, channels), 1)
    head_of = lane // depth
    ones = jnp.ones((2 * tile, channels), BF16)

    def project(form, w, g):
        rows = kv[form, pl.ds(batch * g, batch)].reshape(2 * batch * tile, channels)
        return nn(rows, w[:, channels : 3 * channels]).astype(BF16)

    def attend(form, w, g):
        held = pl.ds(batch * g, batch)
        both = projected[g] if form == 0 else project(form, w, g)
        rows = q[form, held].reshape(batch * tile, channels)
        queries = nn(rows, w[:, :channels]) * scale
        for i in range(batch):
            a = batch * g + i
            keys = both[2 * i * tile : 2 * (i + 1) * tile, :channels]
            values = both[2 * i * tile : 2 * (i + 1) * tile, channels:]
            query = queries[i * tile : (i + 1) * tile]
            chosen = [jnp.where(head_of == h, query, 0.0).astype(BF16) for h in range(heads)]
            scores = nt(jnp.concatenate(chosen, axis=0), keys)
            stats = jnp.zeros((tile, channels), F32)
            probs = []
            for h in range(heads):
                part = scores[h * tile : (h + 1) * tile] + bias[form, h]
                peak = jnp.max(part, axis=1, keepdims=True)
                probs.append(jnp.exp2(part - peak).astype(BF16))
                stats = jnp.where(lane == h, peak, stats)
            totals = nn(jnp.concatenate(probs, axis=0), jnp.concatenate([values, ones], axis=1))
            numer = jnp.zeros((tile, channels), F32)
            for h in range(heads):
                part = totals[h * tile : (h + 1) * tile]
                numer = jnp.where(head_of == h, part[:, :channels], numer)
                stats = jnp.where(lane == heads + h, part[:, channels:], stats)
            pn[form, a] = numer.T.astype(BF16)
            pst[form, a] = stats.T[: 2 * heads]

    def send_partial(form, a):
        if form == 0:
            to, b = lax.rem(a // per, deep), lax.rem(a, per)
            pairs = (rsn.at[lane_z, b], rsn_sem), (rss.at[lane_z, b], rss_sem)
            here, row, col = to == lane_z, r, lap * deep + to
        else:
            pairs = (ren.at[core, chip], ren_sem.at[core]), (res.at[core, chip], res_sem.at[core])
            here, row, col = a == r, a, c
        either(here, pn.at[form, a], pairs[0][0], spn.at[form], pairs[0][1], row, col)
        either(here, pst.at[form, a], pairs[1][0], sps.at[form], pairs[1][1], row, col)

    def send_twin_partial(g):
        @pl.when(g // side != lap)
        def _():
            rows, slot = pl.ds(batch * g, batch), lax.rem(g, side)
            remote(pn.at[0, rows], twn.at[slot], spn.at[0], twn_sem.at[slot], r, twin).start()
            remote(pst.at[0, rows], tws.at[slot], sps.at[0], tws_sem.at[slot], r, twin).start()

    def merge_twin(slot):
        landed(twn.at[slot], twn_sem.at[slot])
        landed(tws.at[slot], tws_sem.at[slot])
        for k in range(batch):
            a = batch * (lap * side + slot) + k
            numer, largest, denom = combine([pn[0, a], twn[slot, k]], [pst[0, a], tws[slot, k]])
            pn[0, a] = jnp.concatenate(numer, axis=0).astype(BF16)
            pst[0, a, :heads] = largest
            pst[0, a, heads:] = denom
            send_partial(0, a)

    def combine(parts, stats):
        peaks = [s[:heads] for s in stats]
        largest = functools.reduce(jnp.maximum, peaks)
        factors = [jnp.exp2(p - largest) for p in peaks]
        denom = sum(f * s[heads:] for f, s in zip(factors, stats))
        rows = []
        for h in range(heads):
            pick = slice(h * depth, (h + 1) * depth)
            rows.append(sum(f[h : h + 1] * p[pick].astype(F32) for f, p in zip(factors, parts)))
        return rows, largest, denom

    def divided(parts, stats):
        rows, _, denom = combine(parts, stats)
        return jnp.concatenate([row / denom[h : h + 1] for h, row in enumerate(rows)], axis=0)

    def run_form(form, w):
        if form == 0:
            def ahead(b, carry):
                g = group(0, b)
                forward_copy(0, g).wait_recv()
                projected[g] = project(0, w, g)
                return carry

            level_to_twin(0)
            ahead(0, 0)
            level_to_twin(1)
            ahead(1, 0)
            level_to_twin(2)
            ahead(2, 0)
            level_to_twin(3)
            ahead(3, 0)
            spread(1, x, r)
        else:
            forward(form, 0)

        def step(b, carry):
            g = group(form, b)
            if form == 0:
                @pl.when(b == 0)
                def _():
                    spread_facing(1)
                relay(1, b)
            if form == 0:
                near_landed(form, g)
            else:
                @pl.when(b + 1 < groups)
                def _():
                    forward(form, b + 1)
                gather_landed(form, g)
                forward_copy(form, g).wait_recv()
            attend(form, w, g)
            if form == 0:
                send_twin_partial(g)
            else:
                for k in range(batch):
                    send_partial(1, batch * g + k)
                @pl.when((b >= MERGE) & (b < MERGE + groups // 2))
                def _():
                    merge_twin(b - MERGE)
            return carry

        lax.fori_loop(0, groups, step, 0)

    def gate(form, rows, mask):
        return jax.nn.sigmoid(nt(wgt[form], rows)) * mask

    def finish(gates, attended, weight):
        gated = gates * attended
        return nn(gated.T.astype(BF16), weight).astype(BF16)

    run_form(0, ws)
    bias_swap.wait_recv()
    for source, cols_at, t in ((be, mine, r), (be_in, other, mate)):
        row = penalty(t)
        for h in range(heads):
            bias[1, h, :, cols_at] = (source[h].astype(F32).T + row) * LOG2E


    run_form(1, we)

    def mask_scalar(k, a):
        at = offs[k] + a
        return tms[at // tile, lax.rem(at, tile)].astype(F32)

    gates_s = [gate(0, q[0, per * c + b], mask_row(r) * mask_scalar(0, per * c + b)) for b in range(per)]
    gates_e = [gate(1, x[1, e], mask_row(2 * c + e) * mask_scalar(1, r)) for e in range(2)]
    landed(rsn, rsn_sem)
    landed(rss, rss_sem)
    for b in range(per):
        attended = divided([rsn[g, b] for g in range(deep)], [rss[g, b] for g in range(deep)])
        out_s[b] = finish(gates_s[b], attended, wso[...])

    for e in range(2):
        landed(ren.at[e], ren_sem.at[e])
        landed(res.at[e], res_sem.at[e])
        attended = divided([ren[e, m] for m in range(nc)], [res[e, m] for m in range(nc)])
        out_e[0, e * tile : (e + 1) * tile, :] = finish(gates_e[e], attended, weo[...])

    bias_swap.wait_send()
    gone(scat.at[pl.ds(0, nc - 1)], ss)
    for form in range(2):
        gone(q.at[0, pl.ds(0, n - 1), part(0)], sa.at[form])
        gone(q.at[0], sg.at[form])
        gone(q.at[0, pl.ds(0, (nc - 1) * per)], sc.at[form])
        gone(q.at[0], sf.at[form])
        remote_count = n - per if form == 0 else n - 1
        gone(pn.at[form, pl.ds(0, remote_count)], spn.at[form])
        gone(pst.at[form, pl.ds(0, remote_count)], sps.at[form])


def local(z_rows, z_cols, bias_start, bias_end, w_start_in, w_start_out, w_end_in, w_end_out, token_mask, offsets):
    n, nc = lax.axis_size("row"), lax.axis_size("col")
    heads, tile, span = bias_start.shape
    channels = z_rows.shape[2]
    per = n // nc
    groups = n // min(BATCH, n)
    vmem = pl.BlockSpec(memory_space=pltpu.VMEM)
    smem = pl.BlockSpec(memory_space=pltpu.SMEM)
    dma = pltpu.SemaphoreType.DMA
    return pl.pallas_call(
        functools.partial(kernel, n, nc, heads),
        out_shape=(
            jax.ShapeDtypeStruct((per, tile, channels), BF16),
            jax.ShapeDtypeStruct((1, span, channels), BF16),
        ),
        in_specs=[pl.BlockSpec(memory_space=pl.ANY)] * 9 + [smem],
        out_specs=(vmem, vmem),
        scratch_shapes=[
            pltpu.VMEM(z_rows.shape, BF16),
            pltpu.VMEM(z_cols.shape, BF16),
            pltpu.VMEM(bias_start.shape, BF16),
            pltpu.VMEM((heads, tile, tile), BF16),
            pltpu.VMEM(w_start_in.shape, BF16),
            pltpu.VMEM(w_start_out.shape, BF16),
            pltpu.VMEM(w_end_in.shape, BF16),
            pltpu.VMEM(w_end_out.shape, BF16),
            pltpu.VMEM((n, tile), jnp.int32),
            pltpu.SMEM((n, tile), jnp.int32),
            dma((10,)),
            pltpu.VMEM((2, 2, tile, channels), BF16),
            pltpu.VMEM((2, 2, tile, channels), BF16),
            pltpu.VMEM((nc, 2, 2, tile // nc, channels), BF16),
            pltpu.VMEM((2, n, 2, tile, channels), BF16),
            pltpu.VMEM((2, n, tile, channels), BF16),
            pltpu.VMEM((2, heads, tile, span), F32),
            pltpu.VMEM((2, channels, channels), BF16),
            pltpu.VMEM((heads, tile, tile), BF16),
            pltpu.VMEM((2, n, channels, tile), BF16),
            pltpu.VMEM((2, n, 2 * heads, tile), F32),
            pltpu.VMEM((nc // 2, per, channels, tile), BF16),
            pltpu.VMEM((nc // 2, per, 2 * heads, tile), F32),
            pltpu.VMEM((2, nc, channels, tile), BF16),
            pltpu.VMEM((2, nc, 2 * heads, tile), F32),
            pltpu.VMEM((groups // 2, n // groups, channels, tile), BF16),
            pltpu.VMEM((groups // 2, n // groups, 2 * heads, tile), F32),
            pltpu.VMEM((groups, n // groups * span, 2 * channels), BF16),
            dma, dma((2,)), dma((2,)), dma((2,)), dma((2,)), dma((2,)), dma((2,)), dma,
            dma, dma((2, groups)), dma((2, groups)), dma((2,)), dma((2, groups)), dma((2, groups)), dma((2, groups)),
            dma, dma, dma((2,)), dma((2,)), dma((groups // 2,)), dma((groups // 2,)), dma,
        ],
        compiler_params=pltpu.CompilerParams(
            collective_id=0, has_side_effects=True, vmem_limit_bytes=62 * 1024 * 1024
        ),
        name="triangle_attention",
    )(
        z_rows, z_cols, bias_start, bias_end, w_start_in, w_start_out, w_end_in, w_end_out,
        token_mask.reshape(-1, tile), offsets,
    )


def solution(mesh):
    return jax.shard_map(
        local,
        mesh=mesh,
        in_specs=(
            P("row", "col", None),
            P("row", "col", None),
            P(None, "row", "col"),
            P(None, "row", "col"),
            P(),
            P(),
            P(),
            P(),
            P(),
            P(),
        ),
        out_specs=(P("col", "row", None), P("row", "col", None)),
        check_vma=False,
    )
```

```python
import functools
import math

import jax
import jax.numpy as jnp
from jax import lax
from jax.experimental import pallas as pl
from jax.experimental.pallas import tpu as pltpu
from jax.sharding import PartitionSpec as P

MESH = pl.DeviceIdType.MESH
LOG2E = math.log2(math.e)
BATCH = 4
MERGE = 2
F32 = jnp.float32
BF16 = jnp.bfloat16


def nn(a, b):
    return lax.dot_general(a, b, (((1,), (0,)), ((), ())), preferred_element_type=F32)


def nt(a, b):
    return lax.dot_general(a, b, (((1,), (1,)), ((), ())), preferred_element_type=F32)


def normalize(block):
    values = block.astype(F32)
    center = values - jnp.mean(values, axis=-1, keepdims=True)
    spread = jnp.mean(center * center, axis=-1, keepdims=True)
    return (center * lax.rsqrt(spread + 1e-05)).astype(BF16)


def kernel(
    n, nc, heads,
    zr_in, zc_in, bs_in, be_far, ws_in, wso_in, we_in, weo_in, tm_in, offs,
    out_s, out_e,
    zr, zc, bs, be, ws, wso, we, weo, tm, tms, got,
    x, across, scat, kv, q, bias, wgt, be_in, pn, pst, rsn, rss, ren, res, twn, tws, projected,
    ss, sa, sg, sc, sf, spn, sps, sb,
    rs, ra, rg, ry, rt, rn, rf, rsn_sem, rss_sem, ren_sem, res_sem, twn_sem, tws_sem, rb,
):
    r = lax.axis_index("row")
    c = lax.axis_index("col")
    core = lax.rem(r, 2)
    chip = r // 2
    mate = r + 1 - 2 * core
    tile = tm.shape[1]
    channels = zr.shape[2]
    batch = min(BATCH, n)
    depth = channels // heads
    per = n // nc
    mine = pl.ds(pl.multiple_of(core * tile, tile), tile)
    other = pl.ds(pl.multiple_of((1 - core) * tile, tile), tile)
    deep = nc // 2
    lap, lane_z = c // deep, lax.rem(c, deep)
    twin = (1 - lap) * deep + lane_z

    def level(d):
        return lap * deep + lax.rem(lane_z + d, deep)

    groups = n // batch
    piece = tile // nc
    block = chip // 2
    facing = r + 2 - 4 * lax.rem(chip, 2)

    side = groups // 2
    spans = [3, 1, 2, 0] if groups == 4 else [k % groups for k in range(1, groups + 1)]

    def group(form, b):
        if form == 0:
            return lax.rem(block + groups - b, groups)
        span = spans[0]
        for k in range(1, groups):
            span = jnp.where(b == k, spans[k], span)
        return lax.rem(block + groups - span, groups)

    def along(u):
        return 2 * lax.rem(block + u // 2, groups) + lax.rem(chip + u, 2)

    def mask_row(t):
        return tm[pl.ds(t, 1), :].astype(F32)

    def penalty(t):
        return (mask_row(t) - 1.0) * 1e9

    def part(p):
        return pl.ds(pl.multiple_of(p * piece, piece), piece)

    fetches = [
        pltpu.make_async_copy(src, dst, got.at[k])
        for k, (src, dst) in enumerate((
            (zr_in, zr), (zc_in, zc), (ws_in, ws), (we_in, we), (tm_in, tm), (bs_in, bs),
            (be_far.at[:, :, mine], be), (wso_in, wso), (weo_in, weo), (tm_in, tms),
        ))
    ]
    for fetch in fetches[:2]:
        fetch.start()

    barrier = pltpu.get_barrier_semaphore()

    def greet(row, col):
        pl.semaphore_signal(barrier, inc=1, device_id=(row, col), device_id_type=MESH)

    def greet_row(d, carry):
        greet(lax.rem(r + d, n), c)
        return carry

    def greet_col(d, carry):
        greet(r, lax.rem(c + d, nc))
        return carry

    for d in sorted(range(1, n), key=lambda d: -min(d, n - d)):
        greet_row(d, 0)
    for d in sorted(range(1, nc), key=lambda d: -min(d, nc - d)):
        greet_col(d, 0)

    for fetch in fetches[2:]:
        fetch.start()

    fetches[0].wait()
    x[0] = normalize(zr[0]).reshape(2, tile, channels)
    fetches[1].wait()
    x[1] = normalize(zc[0]).reshape(2, tile, channels)
    for form in range(2):
        for e in range(2):
            scat[c, form, e] = x[form, e, part(c), :]

    pl.semaphore_wait(barrier, n - 1 + nc - 1)

    def remote(src, dst, send, recv, row, col):
        return pltpu.make_async_remote_copy(
            src_ref=src, dst_ref=dst, send_sem=send, recv_sem=recv,
            device_id=(row, col), device_id_type=MESH,
        )

    def either(here, src, dst, send, recv, row, col):
        @pl.when(here)
        def _():
            pltpu.make_async_copy(src, dst, recv).start()
        @pl.when(jnp.logical_not(here))
        def _():
            remote(src, dst, send, recv, row, col).start()

    bias_swap = remote(
        be_far.at[:, :, other], be_in, sb, rb, mate, c
    )

    def landed(dst, recv):
        remote(dst, dst, sb, recv, mate, c).wait_recv()

    def gone(src, send):
        remote(src, src, send, rb, mate, c).wait_send()

    def scatter(d, carry):
        to = lax.rem(c + d, nc)
        remote(x.at[:, :, part(to)], scat.at[c], ss, rs, r, to).start()
        return carry

    def cross(form):
        def step(u, carry):
            to = along(u)
            for e in range(2):
                dst = q.at[0, r, part(c)] if form == 0 else kv.at[1, r, e, part(c)]
                src = scat.at[to, form, e]
                either((u == 0) & (core == e), src, dst, sa.at[form], ra.at[form, block], 2 * to + e, c)
            return carry
        lax.fori_loop(0, nc, step, 0)

    def near_piece(form, g, p):
        rows = pl.ds(batch * g, batch)
        return q.at[0, rows, part(p)] if form == 0 else kv.at[1, rows, core, part(p)]

    def near_twin(form, b):
        g = group(form, b)
        landed(q.at[0, pl.ds(0, batch), part(0)], ra.at[form, g])
        own = near_piece(form, g, c)
        remote(own, own, sc.at[form], rt.at[form, g], r, twin).start()

    def near_levels(form, b, held):
        g = group(form, b)
        piece_ref = near_piece(form, g, held)
        for d in range(1, deep):
            remote(piece_ref, piece_ref, sc.at[form], rn.at[form, g], r, level(d)).start()

    def relay(form, b):
        landed(near_piece(form, group(form, b), twin), rt.at[form, group(form, b)])
        near_levels(form, b, twin)

    def send_facing(form):
        remote(x.at[form], across.at[form], sg.at[form], ry.at[form], facing, c).start()

    def spread(form, held, row):
        for k in range(groups) if form == 0 else spans:
            to = 4 * lax.rem(block + k, groups) + 2 * lax.rem(chip, 2)
            for e in range(2):
                dst = kv.at[0, row, e] if form == 0 else q.at[1, row]
                recv = rg.at[form, block]
                if k == 0:
                    either(core == e, held.at[form, e], dst, sg.at[form], recv, to + e, c)
                else:
                    remote(held.at[form, e], dst, sg.at[form], recv, to + e, c).start()

    def spread_facing(form):
        landed(x.at[form], ry.at[form])
        spread(form, across, facing)

    def forward_copy(form, g):
        held = kv.at[form, pl.ds(batch * g, batch), core]
        return remote(held, held, sf.at[form], rf.at[form, g], mate, c)

    def near_landed(form, g):
        if form == 0:
            landed(q.at[0, pl.ds(0, batch // 2)], rn.at[form, g])
        elif deep > 1:
            landed(q.at[0, pl.ds(0, (nc - 2) * batch // nc)], rn.at[form, g])

    def gather_landed(form, g):
        landed(q.at[0, pl.ds(0, batch)], rg.at[form, g])

    def forward(form, b):
        (gather_landed if form == 0 else near_landed)(form, group(form, b))
        forward_copy(form, group(form, b)).start()

    lax.fori_loop(1, nc, scatter, 0)
    send_facing(0)
    spread(0, x, r)
    bias_swap.start()

    for fetch in fetches[2:]:
        fetch.wait()
    for form, w in enumerate((ws, we)):
        wgt[form] = w[:, 3 * channels : 4 * channels].astype(F32).T.astype(BF16)

    key_bias = jnp.concatenate([penalty(2 * c), penalty(2 * c + 1)], axis=1)
    for h in range(heads):
        bias[0, h] = (bs[h].astype(F32) + key_bias) * LOG2E

    landed(scat.at[pl.ds(0, nc - 1)], rs)
    cross(0)
    cross(1)
    spread_facing(0)
    send_facing(1)

    def near_level(b, carry):
        g = group(0, b)
        landed(q.at[0, pl.ds(0, batch), part(0)], ra.at[0, g])
        own = near_piece(0, g, c)
        for d in range(1, deep):
            remote(own, own, sc.at[0], rt.at[0, g], r, level(d)).start()
        remote(own, own, sc.at[0], rn.at[0, g], r, twin).start()
        return carry

    def level_to_twin(b):
        g = group(0, b)
        landed(q.at[0, pl.ds(0, (deep - 1) * batch), part(0)], rt.at[0, g])
        for d in range(1, deep):
            held = near_piece(0, g, level(d))
            remote(held, held, sc.at[0], rn.at[0, g], r, twin).start()

    def forward_rows(b, carry):
        forward(0, b)
        return carry

    lax.fori_loop(0, groups, near_level, 0)
    lax.fori_loop(0, groups, forward_rows, 0)
    for b in range(groups):
        near_twin(1, b)
    for b in range(groups):
        near_levels(1, b, c)

    scale = depth ** (-0.5) * LOG2E
    lane = lax.broadcasted_iota(jnp.int32, (tile, channels), 1)
    head_of = lane // depth
    ones = jnp.ones((2 * tile, channels), BF16)

    def project(form, w, g):
        rows = kv[form, pl.ds(batch * g, batch)].reshape(2 * batch * tile, channels)
        return nn(rows, w[:, channels : 3 * channels]).astype(BF16)

    def attend(form, w, g):
        held = pl.ds(batch * g, batch)
        both = projected[g] if form == 0 else project(form, w, g)
        rows = q[form, held].reshape(batch * tile, channels)
        queries = nn(rows, w[:, :channels]) * scale
        for i in range(batch):
            a = batch * g + i
            keys = both[2 * i * tile : 2 * (i + 1) * tile, :channels]
            values = both[2 * i * tile : 2 * (i + 1) * tile, channels:]
            query = queries[i * tile : (i + 1) * tile]
            chosen = [jnp.where(head_of == h, query, 0.0).astype(BF16) for h in range(heads)]
            scores = nt(jnp.concatenate(chosen, axis=0), keys)
            stats = jnp.zeros((tile, channels), F32)
            probs = []
            for h in range(heads):
                part = scores[h * tile : (h + 1) * tile] + bias[form, h]
                peak = jnp.max(part, axis=1, keepdims=True)
                probs.append(jnp.exp2(part - peak).astype(BF16))
                stats = jnp.where(lane == h, peak, stats)
            totals = nn(jnp.concatenate(probs, axis=0), jnp.concatenate([values, ones], axis=1))
            numer = jnp.zeros((tile, channels), F32)
            for h in range(heads):
                part = totals[h * tile : (h + 1) * tile]
                numer = jnp.where(head_of == h, part[:, :channels], numer)
                stats = jnp.where(lane == heads + h, part[:, channels:], stats)
            pn[form, a] = numer.T.astype(BF16)
            pst[form, a] = stats.T[: 2 * heads]

    def send_partial(form, a):
        if form == 0:
            to, b = lax.rem(a // per, deep), lax.rem(a, per)
            pairs = (rsn.at[lane_z, b], rsn_sem), (rss.at[lane_z, b], rss_sem)
            here, row, col = to == lane_z, r, lap * deep + to
        else:
            pairs = (ren.at[core, chip], ren_sem.at[core]), (res.at[core, chip], res_sem.at[core])
            here, row, col = a == r, a, c
        either(here, pn.at[form, a], pairs[0][0], spn.at[form], pairs[0][1], row, col)
        either(here, pst.at[form, a], pairs[1][0], sps.at[form], pairs[1][1], row, col)

    def send_twin_partial(g):
        @pl.when(g // side != lap)
        def _():
            rows, slot = pl.ds(batch * g, batch), lax.rem(g, side)
            remote(pn.at[0, rows], twn.at[slot], spn.at[0], twn_sem.at[slot], r, twin).start()
            remote(pst.at[0, rows], tws.at[slot], sps.at[0], tws_sem.at[slot], r, twin).start()

    def merge_twin(slot):
        landed(twn.at[slot], twn_sem.at[slot])
        landed(tws.at[slot], tws_sem.at[slot])
        for k in range(batch):
            a = batch * (lap * side + slot) + k
            numer, largest, denom = combine([pn[0, a], twn[slot, k]], [pst[0, a], tws[slot, k]])
            pn[0, a] = jnp.concatenate(numer, axis=0).astype(BF16)
            pst[0, a, :heads] = largest
            pst[0, a, heads:] = denom
            send_partial(0, a)

    def combine(parts, stats):
        peaks = [s[:heads] for s in stats]
        largest = functools.reduce(jnp.maximum, peaks)
        factors = [jnp.exp2(p - largest) for p in peaks]
        denom = sum(f * s[heads:] for f, s in zip(factors, stats))
        rows = []
        for h in range(heads):
            pick = slice(h * depth, (h + 1) * depth)
            rows.append(sum(f[h : h + 1] * p[pick].astype(F32) for f, p in zip(factors, parts)))
        return rows, largest, denom

    def divided(parts, stats):
        rows, _, denom = combine(parts, stats)
        return jnp.concatenate([row / denom[h : h + 1] for h, row in enumerate(rows)], axis=0)

    def prepare_ending_bias():
        bias_swap.wait_recv()
        for source, cols_at, t in ((be, mine, r), (be_in, other, mate)):
            row = penalty(t)
            for h in range(heads):
                bias[1, h, :, cols_at] = (source[h].astype(F32).T + row) * LOG2E

    def run_form(form, w):
        if form == 0:
            def ahead(b, carry):
                g = group(0, b)
                forward_copy(0, g).wait_recv()
                projected[g] = project(0, w, g)
                return carry

            level_to_twin(0)
            ahead(0, 0)
            level_to_twin(1)
            ahead(1, 0)
            level_to_twin(2)
            ahead(2, 0)
            level_to_twin(3)
            ahead(3, 0)
            spread(1, x, r)
            prepare_ending_bias()
        else:
            forward(form, 0)

        def step(b, carry):
            g = group(form, b)
            if form == 0:
                @pl.when(b == 0)
                def _():
                    spread_facing(1)
                relay(1, b)
            if form == 0:
                near_landed(form, g)
            else:
                @pl.when(b + 1 < groups)
                def _():
                    forward(form, b + 1)
                gather_landed(form, g)
                forward_copy(form, g).wait_recv()
            attend(form, w, g)
            if form == 0:
                send_twin_partial(g)
            else:
                @pl.when(b + 1 < groups)
                def _():
                    for k in range(batch):
                        a = batch * g + k
                        remote(pn.at[1, a], ren.at[core, chip], spn.at[1], ren_sem.at[core], a, c).start()
                        remote(pst.at[1, a], res.at[core, chip], sps.at[1], res_sem.at[core], a, c).start()
                @pl.when(b + 1 == groups)
                def _():
                    for k in range(batch):
                        send_partial(1, batch * g + k)
                @pl.when((b >= MERGE) & (b < MERGE + groups // 2))
                def _():
                    merge_twin(b - MERGE)
            return carry

        lax.fori_loop(0, groups, step, 0)

    def gate(form, rows, mask):
        return jax.nn.sigmoid(nt(wgt[form], rows)) * mask

    def finish(gates, attended, weight):
        gated = gates * attended
        return nn(gated.T.astype(BF16), weight).astype(BF16)

    run_form(0, ws)
    run_form(1, we)

    def mask_scalar(k, a):
        at = offs[k] + a
        return tms[at // tile, lax.rem(at, tile)].astype(F32)

    gates_s = [gate(0, q[0, per * c + b], mask_row(r) * mask_scalar(0, per * c + b)) for b in range(per)]
    gates_e = [gate(1, x[1, e], mask_row(2 * c + e) * mask_scalar(1, r)) for e in range(2)]
    landed(rsn, rsn_sem)
    landed(rss, rss_sem)
    for b in range(per):
        attended = divided([rsn[g, b] for g in range(deep)], [rss[g, b] for g in range(deep)])
        out_s[b] = finish(gates_s[b], attended, wso[...])

    for e in range(2):
        landed(ren.at[e], ren_sem.at[e])
        landed(res.at[e], res_sem.at[e])
        attended = divided([ren[e, m] for m in range(nc)], [res[e, m] for m in range(nc)])
        out_e[0, e * tile : (e + 1) * tile, :] = finish(gates_e[e], attended, weo[...])

    bias_swap.wait_send()
    gone(scat.at[pl.ds(0, nc - 1)], ss)
    for form in range(2):
        gone(q.at[0, pl.ds(0, n - 1), part(0)], sa.at[form])
        gone(q.at[0], sg.at[form])
        gone(q.at[0, pl.ds(0, (nc - 1) * per)], sc.at[form])
        gone(q.at[0], sf.at[form])
        remote_count = n - per if form == 0 else n - 1
        gone(pn.at[form, pl.ds(0, remote_count)], spn.at[form])
        gone(pst.at[form, pl.ds(0, remote_count)], sps.at[form])


def local(z_rows, z_cols, bias_start, bias_end, w_start_in, w_start_out, w_end_in, w_end_out, token_mask, offsets):
    n, nc = lax.axis_size("row"), lax.axis_size("col")
    heads, tile, span = bias_start.shape
    channels = z_rows.shape[2]
    per = n // nc
    groups = n // min(BATCH, n)
    vmem = pl.BlockSpec(memory_space=pltpu.VMEM)
    smem = pl.BlockSpec(memory_space=pltpu.SMEM)
    dma = pltpu.SemaphoreType.DMA
    return pl.pallas_call(
        functools.partial(kernel, n, nc, heads),
        out_shape=(
            jax.ShapeDtypeStruct((per, tile, channels), BF16),
            jax.ShapeDtypeStruct((1, span, channels), BF16),
        ),
        in_specs=[pl.BlockSpec(memory_space=pl.ANY)] * 9 + [smem],
        out_specs=(vmem, vmem),
        scratch_shapes=[
            pltpu.VMEM(z_rows.shape, BF16),
            pltpu.VMEM(z_cols.shape, BF16),
            pltpu.VMEM(bias_start.shape, BF16),
            pltpu.VMEM((heads, tile, tile), BF16),
            pltpu.VMEM(w_start_in.shape, BF16),
            pltpu.VMEM(w_start_out.shape, BF16),
            pltpu.VMEM(w_end_in.shape, BF16),
            pltpu.VMEM(w_end_out.shape, BF16),
            pltpu.VMEM((n, tile), jnp.int32),
            pltpu.SMEM((n, tile), jnp.int32),
            dma((10,)),
            pltpu.VMEM((2, 2, tile, channels), BF16),
            pltpu.VMEM((2, 2, tile, channels), BF16),
            pltpu.VMEM((nc, 2, 2, tile // nc, channels), BF16),
            pltpu.VMEM((2, n, 2, tile, channels), BF16),
            pltpu.VMEM((2, n, tile, channels), BF16),
            pltpu.VMEM((2, heads, tile, span), F32),
            pltpu.VMEM((2, channels, channels), BF16),
            pltpu.VMEM((heads, tile, tile), BF16),
            pltpu.VMEM((2, n, channels, tile), BF16),
            pltpu.VMEM((2, n, 2 * heads, tile), F32),
            pltpu.VMEM((nc // 2, per, channels, tile), BF16),
            pltpu.VMEM((nc // 2, per, 2 * heads, tile), F32),
            pltpu.VMEM((2, nc, channels, tile), BF16),
            pltpu.VMEM((2, nc, 2 * heads, tile), F32),
            pltpu.VMEM((groups // 2, n // groups, channels, tile), BF16),
            pltpu.VMEM((groups // 2, n // groups, 2 * heads, tile), F32),
            pltpu.VMEM((groups, n // groups * span, 2 * channels), BF16),
            dma, dma((2,)), dma((2,)), dma((2,)), dma((2,)), dma((2,)), dma((2,)), dma,
            dma, dma((2, groups)), dma((2, groups)), dma((2,)), dma((2, groups)), dma((2, groups)), dma((2, groups)),
            dma, dma, dma((2,)), dma((2,)), dma((groups // 2,)), dma((groups // 2,)), dma,
        ],
        compiler_params=pltpu.CompilerParams(
            collective_id=0, has_side_effects=True, vmem_limit_bytes=62 * 1024 * 1024
        ),
        name="triangle_attention",
    )(
        z_rows, z_cols, bias_start, bias_end, w_start_in, w_start_out, w_end_in, w_end_out,
        token_mask.reshape(-1, tile), offsets,
    )


def solution(mesh):
    return jax.shard_map(
        local,
        mesh=mesh,
        in_specs=(
            P("row", "col", None),
            P("row", "col", None),
            P(None, "row", "col"),
            P(None, "row", "col"),
            P(),
            P(),
            P(),
            P(),
            P(),
            P(),
        ),
        out_specs=(P("col", "row", None), P("row", "col", None)),
        check_vma=False,
    )
```

```python
import functools
import math

import jax
import jax.numpy as jnp
from jax import lax
from jax.experimental import pallas as pl
from jax.experimental.pallas import tpu as pltpu
from jax.sharding import PartitionSpec as P

MESH = pl.DeviceIdType.MESH
LOG2E = math.log2(math.e)
BATCH = 4
MERGE = 2
F32 = jnp.float32
BF16 = jnp.bfloat16


def nn(a, b):
    return lax.dot_general(a, b, (((1,), (0,)), ((), ())), preferred_element_type=F32)


def nt(a, b):
    return lax.dot_general(a, b, (((1,), (1,)), ((), ())), preferred_element_type=F32)


def normalize(block):
    values = block.astype(F32)
    center = values - jnp.mean(values, axis=-1, keepdims=True)
    spread = jnp.mean(center * center, axis=-1, keepdims=True)
    return (center * lax.rsqrt(spread + 1e-05)).astype(BF16)


def kernel(
    n, nc, heads,
    zr_in, zc_in, bs_in, be_far, ws_in, wso_in, we_in, weo_in, tm_in, offs,
    out_s, out_e,
    zr, zc, bs, be, ws, wso, we, weo, tm, tms, got,
    x, across, scat, kv, q, bias, wgt, be_in, pn, pst, rsn, rss, ren, res, twn, tws, projected,
    ss, sa, sg, sc, sf, spn, sps, sb,
    rs, ra, rg, ry, rt, rn, rf, rsn_sem, rss_sem, ren_sem, res_sem, twn_sem, tws_sem, rb,
):
    r = lax.axis_index("row")
    c = lax.axis_index("col")
    core = lax.rem(r, 2)
    chip = r // 2
    mate = r + 1 - 2 * core
    tile = tm.shape[1]
    channels = zr.shape[2]
    batch = min(BATCH, n)
    depth = channels // heads
    per = n // nc
    mine = pl.ds(pl.multiple_of(core * tile, tile), tile)
    other = pl.ds(pl.multiple_of((1 - core) * tile, tile), tile)
    deep = nc // 2
    lap, lane_z = c // deep, lax.rem(c, deep)
    twin = (1 - lap) * deep + lane_z

    def level(d):
        return lap * deep + lax.rem(lane_z + d, deep)

    groups = n // batch
    piece = tile // nc
    block = chip // 2
    facing = r + 2 - 4 * lax.rem(chip, 2)

    side = groups // 2
    spans = [3, 1, 2, 0] if groups == 4 else [k % groups for k in range(1, groups + 1)]

    def group(form, b):
        if form == 0:
            return lax.rem(block + groups - b, groups)
        span = spans[0]
        for k in range(1, groups):
            span = jnp.where(b == k, spans[k], span)
        return lax.rem(block + groups - span, groups)

    def along(u):
        return 2 * lax.rem(block + u // 2, groups) + lax.rem(chip + u, 2)

    def mask_row(t):
        return tm[pl.ds(t, 1), :].astype(F32)

    def penalty(t):
        return (mask_row(t) - 1.0) * 1e9

    def part(p):
        return pl.ds(pl.multiple_of(p * piece, piece), piece)

    fetches = [
        pltpu.make_async_copy(src, dst, got.at[k])
        for k, (src, dst) in enumerate((
            (zr_in, zr), (zc_in, zc), (ws_in, ws), (we_in, we), (tm_in, tm), (bs_in, bs),
            (be_far.at[:, :, mine], be), (wso_in, wso), (weo_in, weo), (tm_in, tms),
        ))
    ]
    for fetch in fetches[:2]:
        fetch.start()

    barrier = pltpu.get_barrier_semaphore()

    def greet(row, col):
        pl.semaphore_signal(barrier, inc=1, device_id=(row, col), device_id_type=MESH)

    def greet_row(d, carry):
        greet(lax.rem(r + d, n), c)
        return carry

    def greet_col(d, carry):
        greet(r, lax.rem(c + d, nc))
        return carry

    for d in sorted(range(1, n), key=lambda d: -min(d, n - d)):
        greet_row(d, 0)
    for d in sorted(range(1, nc), key=lambda d: -min(d, nc - d)):
        greet_col(d, 0)

    for fetch in fetches[2:]:
        fetch.start()

    fetches[0].wait()
    x[0] = normalize(zr[0]).reshape(2, tile, channels)
    fetches[1].wait()
    x[1] = normalize(zc[0]).reshape(2, tile, channels)
    for form in range(2):
        for e in range(2):
            scat[c, form, e] = x[form, e, part(c), :]

    pl.semaphore_wait(barrier, n - 1 + nc - 1)

    def remote(src, dst, send, recv, row, col):
        return pltpu.make_async_remote_copy(
            src_ref=src, dst_ref=dst, send_sem=send, recv_sem=recv,
            device_id=(row, col), device_id_type=MESH,
        )

    def either(here, src, dst, send, recv, row, col):
        @pl.when(here)
        def _():
            pltpu.make_async_copy(src, dst, recv).start()
        @pl.when(jnp.logical_not(here))
        def _():
            remote(src, dst, send, recv, row, col).start()

    bias_swap = remote(
        be_far.at[:, :, other], be_in, sb, rb, mate, c
    )

    def landed(dst, recv):
        remote(dst, dst, sb, recv, mate, c).wait_recv()

    def gone(src, send):
        remote(src, src, send, rb, mate, c).wait_send()

    def scatter(d, carry):
        to = lax.rem(c + d, nc)
        remote(x.at[:, :, part(to)], scat.at[c], ss, rs, r, to).start()
        return carry

    def cross(form):
        def step(u, carry):
            to = along(u)
            for e in range(2):
                dst = q.at[0, r, part(c)] if form == 0 else kv.at[1, r, e, part(c)]
                src = scat.at[to, form, e]
                either((u == 0) & (core == e), src, dst, sa.at[form], ra.at[form, block], 2 * to + e, c)
            return carry
        lax.fori_loop(0, nc, step, 0)

    def near_piece(form, g, p):
        rows = pl.ds(batch * g, batch)
        return q.at[0, rows, part(p)] if form == 0 else kv.at[1, rows, core, part(p)]

    def near_twin(form, b):
        g = group(form, b)
        landed(q.at[0, pl.ds(0, batch), part(0)], ra.at[form, g])
        own = near_piece(form, g, c)
        remote(own, own, sc.at[form], rt.at[form, g], r, twin).start()

    def near_levels(form, b, held):
        g = group(form, b)
        piece_ref = near_piece(form, g, held)
        for d in range(1, deep):
            remote(piece_ref, piece_ref, sc.at[form], rn.at[form, g], r, level(d)).start()

    def relay(form, b):
        landed(near_piece(form, group(form, b), twin), rt.at[form, group(form, b)])
        near_levels(form, b, twin)

    def send_facing(form):
        remote(x.at[form], across.at[form], sg.at[form], ry.at[form], facing, c).start()

    def spread(form, held, row):
        for k in range(groups) if form == 0 else spans:
            to = 4 * lax.rem(block + k, groups) + 2 * lax.rem(chip, 2)
            for e in range(2):
                dst = kv.at[0, row, e] if form == 0 else q.at[1, row]
                recv = rg.at[form, block]
                if k == 0:
                    either(core == e, held.at[form, e], dst, sg.at[form], recv, to + e, c)
                else:
                    remote(held.at[form, e], dst, sg.at[form], recv, to + e, c).start()

    def spread_facing(form):
        landed(x.at[form], ry.at[form])
        spread(form, across, facing)

    def forward_copy(form, g):
        held = kv.at[form, pl.ds(batch * g, batch), core]
        return remote(held, held, sf.at[form], rf.at[form, g], mate, c)

    def near_landed(form, g):
        if form == 0:
            landed(q.at[0, pl.ds(0, batch // 2)], rn.at[form, g])
        elif deep > 1:
            landed(q.at[0, pl.ds(0, (nc - 2) * batch // nc)], rn.at[form, g])

    def gather_landed(form, g):
        landed(q.at[0, pl.ds(0, batch)], rg.at[form, g])

    def forward(form, b):
        (gather_landed if form == 0 else near_landed)(form, group(form, b))
        forward_copy(form, group(form, b)).start()

    lax.fori_loop(1, nc, scatter, 0)
    send_facing(0)
    spread(0, x, r)
    bias_swap.start()

    for fetch in fetches[2:]:
        fetch.wait()
    for form, w in enumerate((ws, we)):
        wgt[form] = w[:, 3 * channels : 4 * channels].astype(F32).T.astype(BF16)

    key_bias = jnp.concatenate([penalty(2 * c), penalty(2 * c + 1)], axis=1)
    for h in range(heads):
        bias[0, h] = (bs[h].astype(F32) + key_bias) * LOG2E

    landed(scat.at[pl.ds(0, nc - 1)], rs)
    cross(0)
    cross(1)
    spread_facing(0)
    send_facing(1)

    def near_level(b, carry):
        g = group(0, b)
        landed(q.at[0, pl.ds(0, batch), part(0)], ra.at[0, g])
        own = near_piece(0, g, c)
        for d in range(1, deep):
            remote(own, own, sc.at[0], rt.at[0, g], r, level(d)).start()
        remote(own, own, sc.at[0], rn.at[0, g], r, twin).start()
        return carry

    def level_to_twin(b):
        g = group(0, b)
        landed(q.at[0, pl.ds(0, (deep - 1) * batch), part(0)], rt.at[0, g])
        for d in range(1, deep):
            held = near_piece(0, g, level(d))
            remote(held, held, sc.at[0], rn.at[0, g], r, twin).start()

    def forward_rows(b, carry):
        forward(0, b)
        return carry

    lax.fori_loop(0, groups, near_level, 0)
    lax.fori_loop(0, groups, forward_rows, 0)
    for b in range(groups):
        near_twin(1, b)
    for b in range(groups):
        near_levels(1, b, c)

    scale = depth ** (-0.5) * LOG2E
    lane = lax.broadcasted_iota(jnp.int32, (tile, channels), 1)
    head_of = lane // depth
    ones = jnp.ones((2 * tile, channels), BF16)

    def project(form, w, g):
        rows = kv[form, pl.ds(batch * g, batch)].reshape(2 * batch * tile, channels)
        return nn(rows, w[:, channels : 3 * channels]).astype(BF16)

    def attend(form, w, g):
        held = pl.ds(batch * g, batch)
        both = projected[g] if form == 0 else project(form, w, g)
        rows = q[form, held].reshape(batch * tile, channels)
        queries = nn(rows, w[:, :channels]) * scale
        for i in range(batch):
            a = batch * g + i
            keys = both[2 * i * tile : 2 * (i + 1) * tile, :channels]
            values = both[2 * i * tile : 2 * (i + 1) * tile, channels:]
            query = queries[i * tile : (i + 1) * tile]
            chosen = [jnp.where(head_of == h, query, 0.0).astype(BF16) for h in range(heads)]
            scores = nt(jnp.concatenate(chosen, axis=0), keys)
            stats = jnp.zeros((tile, channels), F32)
            probs = []
            for h in range(heads):
                part = scores[h * tile : (h + 1) * tile] + bias[form, h]
                peak = jnp.max(part, axis=1, keepdims=True)
                probs.append(jnp.exp2(part - peak).astype(BF16))
                stats = jnp.where(lane == h, peak, stats)
            totals = nn(jnp.concatenate(probs, axis=0), jnp.concatenate([values, ones], axis=1))
            numer = jnp.zeros((tile, channels), F32)
            for h in range(heads):
                part = totals[h * tile : (h + 1) * tile]
                numer = jnp.where(head_of == h, part[:, :channels], numer)
                stats = jnp.where(lane == heads + h, part[:, channels:], stats)
            pn[form, a] = numer.T.astype(BF16)
            pst[form, a] = stats.T[: 2 * heads]

    def send_partial(form, a):
        if form == 0:
            to, b = lax.rem(a // per, deep), lax.rem(a, per)
            pairs = (rsn.at[lane_z, b], rsn_sem), (rss.at[lane_z, b], rss_sem)
            here, row, col = to == lane_z, r, lap * deep + to
        else:
            pairs = (ren.at[core, chip], ren_sem.at[core]), (res.at[core, chip], res_sem.at[core])
            here, row, col = a == r, a, c
        either(here, pn.at[form, a], pairs[0][0], spn.at[form], pairs[0][1], row, col)
        either(here, pst.at[form, a], pairs[1][0], sps.at[form], pairs[1][1], row, col)

    def send_twin_partial(g):
        @pl.when(g // side != lap)
        def _():
            rows, slot = pl.ds(batch * g, batch), lax.rem(g, side)
            remote(pn.at[0, rows], twn.at[slot], spn.at[0], twn_sem.at[slot], r, twin).start()
            remote(pst.at[0, rows], tws.at[slot], sps.at[0], tws_sem.at[slot], r, twin).start()

    def merge_twin(slot):
        landed(twn.at[slot], twn_sem.at[slot])
        landed(tws.at[slot], tws_sem.at[slot])
        for k in range(batch):
            a = batch * (lap * side + slot) + k
            numer, largest, denom = combine([pn[0, a], twn[slot, k]], [pst[0, a], tws[slot, k]])
            pn[0, a] = jnp.concatenate(numer, axis=0).astype(BF16)
            pst[0, a, :heads] = largest
            pst[0, a, heads:] = denom
            send_partial(0, a)

    def combine(parts, stats):
        peaks = [s[:heads] for s in stats]
        largest = functools.reduce(jnp.maximum, peaks)
        factors = [jnp.exp2(p - largest) for p in peaks]
        denom = sum(f * s[heads:] for f, s in zip(factors, stats))
        rows = []
        for h in range(heads):
            pick = slice(h * depth, (h + 1) * depth)
            rows.append(sum(f[h : h + 1] * p[pick].astype(F32) for f, p in zip(factors, parts)))
        return rows, largest, denom

    def divided(parts, stats):
        rows, _, denom = combine(parts, stats)
        return jnp.concatenate([row / denom[h : h + 1] for h, row in enumerate(rows)], axis=0)

    def run_form(form, w):
        if form == 0:
            def ahead(b, carry):
                g = group(0, b)
                forward_copy(0, g).wait_recv()
                projected[g] = project(0, w, g)
                return carry

            level_to_twin(0)
            ahead(0, 0)
            level_to_twin(1)
            ahead(1, 0)
            level_to_twin(2)
            ahead(2, 0)
            level_to_twin(3)
            ahead(3, 0)
            spread(1, x, r)
        else:
            forward(form, 0)

        def step(b, carry):
            g = group(form, b)
            if form == 0:
                relay(1, b)
                @pl.when(b == 1)
                def _():
                    spread_facing(1)
            if form == 0:
                near_landed(form, g)
            else:
                @pl.when(b + 1 < groups)
                def _():
                    forward(form, b + 1)
                gather_landed(form, g)
                forward_copy(form, g).wait_recv()
            attend(form, w, g)
            if form == 0:
                send_twin_partial(g)
            else:
                for k in range(batch):
                    send_partial(1, batch * g + k)
                @pl.when((b >= MERGE) & (b < MERGE + groups // 2))
                def _():
                    merge_twin(b - MERGE)
            return carry

        lax.fori_loop(0, groups, step, 0)

    def gate(form, rows, mask):
        return jax.nn.sigmoid(nt(wgt[form], rows)) * mask

    def finish(gates, attended, weight):
        gated = gates * attended
        return nn(gated.T.astype(BF16), weight).astype(BF16)

    run_form(0, ws)
    bias_swap.wait_recv()
    for source, cols_at, t in ((be, mine, r), (be_in, other, mate)):
        row = penalty(t)
        for h in range(heads):
            bias[1, h, :, cols_at] = (source[h].astype(F32).T + row) * LOG2E


    run_form(1, we)

    def mask_scalar(k, a):
        at = offs[k] + a
        return tms[at // tile, lax.rem(at, tile)].astype(F32)

    gates_s = [gate(0, q[0, per * c + b], mask_row(r) * mask_scalar(0, per * c + b)) for b in range(per)]
    gates_e = [gate(1, x[1, e], mask_row(2 * c + e) * mask_scalar(1, r)) for e in range(2)]
    landed(rsn, rsn_sem)
    landed(rss, rss_sem)
    for b in range(per):
        attended = divided([rsn[g, b] for g in range(deep)], [rss[g, b] for g in range(deep)])
        out_s[b] = finish(gates_s[b], attended, wso[...])

    for e in range(2):
        landed(ren.at[e], ren_sem.at[e])
        landed(res.at[e], res_sem.at[e])
        attended = divided([ren[e, m] for m in range(nc)], [res[e, m] for m in range(nc)])
        out_e[0, e * tile : (e + 1) * tile, :] = finish(gates_e[e], attended, weo[...])

    bias_swap.wait_send()
    gone(scat.at[pl.ds(0, nc - 1)], ss)
    for form in range(2):
        gone(q.at[0, pl.ds(0, n - 1), part(0)], sa.at[form])
        gone(q.at[0], sg.at[form])
        gone(q.at[0, pl.ds(0, (nc - 1) * per)], sc.at[form])
        gone(q.at[0], sf.at[form])
        remote_count = n - per if form == 0 else n - 1
        gone(pn.at[form, pl.ds(0, remote_count)], spn.at[form])
        gone(pst.at[form, pl.ds(0, remote_count)], sps.at[form])


def local(z_rows, z_cols, bias_start, bias_end, w_start_in, w_start_out, w_end_in, w_end_out, token_mask, offsets):
    n, nc = lax.axis_size("row"), lax.axis_size("col")
    heads, tile, span = bias_start.shape
    channels = z_rows.shape[2]
    per = n // nc
    groups = n // min(BATCH, n)
    vmem = pl.BlockSpec(memory_space=pltpu.VMEM)
    smem = pl.BlockSpec(memory_space=pltpu.SMEM)
    dma = pltpu.SemaphoreType.DMA
    return pl.pallas_call(
        functools.partial(kernel, n, nc, heads),
        out_shape=(
            jax.ShapeDtypeStruct((per, tile, channels), BF16),
            jax.ShapeDtypeStruct((1, span, channels), BF16),
        ),
        in_specs=[pl.BlockSpec(memory_space=pl.ANY)] * 9 + [smem],
        out_specs=(vmem, vmem),
        scratch_shapes=[
            pltpu.VMEM(z_rows.shape, BF16),
            pltpu.VMEM(z_cols.shape, BF16),
            pltpu.VMEM(bias_start.shape, BF16),
            pltpu.VMEM((heads, tile, tile), BF16),
            pltpu.VMEM(w_start_in.shape, BF16),
            pltpu.VMEM(w_start_out.shape, BF16),
            pltpu.VMEM(w_end_in.shape, BF16),
            pltpu.VMEM(w_end_out.shape, BF16),
            pltpu.VMEM((n, tile), jnp.int32),
            pltpu.SMEM((n, tile), jnp.int32),
            dma((10,)),
            pltpu.VMEM((2, 2, tile, channels), BF16),
            pltpu.VMEM((2, 2, tile, channels), BF16),
            pltpu.VMEM((nc, 2, 2, tile // nc, channels), BF16),
            pltpu.VMEM((2, n, 2, tile, channels), BF16),
            pltpu.VMEM((2, n, tile, channels), BF16),
            pltpu.VMEM((2, heads, tile, span), F32),
            pltpu.VMEM((2, channels, channels), BF16),
            pltpu.VMEM((heads, tile, tile), BF16),
            pltpu.VMEM((2, n, channels, tile), BF16),
            pltpu.VMEM((2, n, 2 * heads, tile), F32),
            pltpu.VMEM((nc // 2, per, channels, tile), BF16),
            pltpu.VMEM((nc // 2, per, 2 * heads, tile), F32),
            pltpu.VMEM((2, nc, channels, tile), BF16),
            pltpu.VMEM((2, nc, 2 * heads, tile), F32),
            pltpu.VMEM((groups // 2, n // groups, channels, tile), BF16),
            pltpu.VMEM((groups // 2, n // groups, 2 * heads, tile), F32),
            pltpu.VMEM((groups, n // groups * span, 2 * channels), BF16),
            dma, dma((2,)), dma((2,)), dma((2,)), dma((2,)), dma((2,)), dma((2,)), dma,
            dma, dma((2, groups)), dma((2, groups)), dma((2,)), dma((2, groups)), dma((2, groups)), dma((2, groups)),
            dma, dma, dma((2,)), dma((2,)), dma((groups // 2,)), dma((groups // 2,)), dma,
        ],
        compiler_params=pltpu.CompilerParams(
            collective_id=0, has_side_effects=True, vmem_limit_bytes=62 * 1024 * 1024
        ),
        name="triangle_attention",
    )(
        z_rows, z_cols, bias_start, bias_end, w_start_in, w_start_out, w_end_in, w_end_out,
        token_mask.reshape(-1, tile), offsets,
    )


def solution(mesh):
    return jax.shard_map(
        local,
        mesh=mesh,
        in_specs=(
            P("row", "col", None),
            P("row", "col", None),
            P(None, "row", "col"),
            P(None, "row", "col"),
            P(),
            P(),
            P(),
            P(),
            P(),
            P(),
        ),
        out_specs=(P("col", "row", None), P("row", "col", None)),
        check_vma=False,
    )
```
